32 devices in a mesh: grp: 4 (over x, core), mem: 8 (over z, y).
Axes of the slice: x: 2, y: 2, z: 4, core: 2. Of those that a mesh axis runs over, the one named last changes fastest.
Arguments:
- tiles: bfloat16 [4, 32, 64, 4096], P('grp', 'mem'), may hold values from -0.75 to 0.75
- tile_ids: int32 [4, 4, 32], P(None, None, 'mem'), may hold values from 0 to 383, as said below
- occ_blocks: bfloat16 [384, 4096], P('mem'), may hold values from -0.75 to 0.75
- virt_blocks: bfloat16 [384, 2, 4096], P('mem'), may hold values from -0.75 to 0.75
Outputs:
- chi_band: float32 [1024, 768], P(('grp', 'mem'))
The draws below stay inside these ranges and needn't reach their ends.
Inputs may be any that keep to these rules, and one draw needn't show every extreme that they name: tile_ids[g,0,c] is an RI block of the group, below 4; tile_ids[g,1,c] is the first or the last of the row blocks c // 4 * 48 to (c // 4 + 1) * 48 - 1; tile_ids[g,2,c] differs from tile_ids[g,1,c] by at most one; tile_ids[g,3,c] is 1 for a live slot and 0 for an empty one; the live slots of a device come first, every device has one or more, and some device has all 4 live.
All inputs are finite; a program needn't handle non-finite values.
Results may differ from the reference program's by a relative error of at most 0.006.
Values may be sent and summed in bfloat16 or wider, within the bound.
No kernel may reach another device: no remote copies, remote signals or barrier semaphores. Data moves between devices by JAX's collectives and lax.ppermute only.
A program may use at most 128 MiB of HBM per device.

```python
import jax
import jax.numpy as jnp
from jax import lax

BLK = 64
RIB = 4
SLOTS = 4
NB = 384
N_GRP = 4
N_MEM = 8


def draw_tile_ids(key, part):
    columns = N_MEM * SLOTS
    key_side, key_step, key_block, key_count = jax.random.split(key, 4)
    column = jnp.arange(columns, dtype=jnp.int32)
    owner = column // SLOTS
    slot_index = column % SLOTS
    per_owner = NB // N_MEM
    side_pick = jax.random.randint(key_side, (N_GRP, columns), 0, 2)
    row_block = owner[None, :] * per_owner + side_pick * (per_owner - 1)
    step_pick = jax.random.randint(key_step, (N_GRP, columns), -1, 2)
    col_block = jnp.clip(row_block + step_pick, 0, NB - 1)
    ri_block = jax.random.randint(key_block, (N_GRP, columns), 0, RIB)
    live_count = jax.random.randint(key_count, (N_GRP, N_MEM), 1, SLOTS + 1)
    live_count = live_count.at[0, 0].set(SLOTS)
    live_flag = (slot_index[None, :] < live_count[:, owner]).astype(jnp.int32)
    return jnp.stack([ri_block, row_block, col_block, live_flag], axis=1).astype(jnp.int32)


def level_of(rng, dims, cuts, smallest, high):
    gain = 1.0
    for dim, parts in cuts:
        steps = jax.random.uniform(jax.random.fold_in(jax.random.fold_in(rng, 6), dim), (parts,), jnp.float32, smallest / len(cuts), high / len(cuts))
        gain = gain * jnp.repeat(jnp.exp(steps), dims[dim] // parts).reshape((-1,) + (1,) * (len(dims) - 1 - dim))
    return gain


def normal_values(rng, dims, deviation, limit, pieces=(), held_as=jnp.bfloat16):
    values = jax.random.normal(rng, dims, jnp.float32) * deviation
    if len(pieces) > 0:
        values = level_of(rng, dims, pieces, -0.22, 0.18) * values
    return jnp.clip(values, min=-limit, max=limit).astype(held_as)


def setup_inputs(seed: int = 0) -> dict:
    keys = jax.random.split(jax.random.key(seed), 5)
    return {
        "tiles": normal_values(keys[0], (N_GRP, N_MEM * SLOTS, BLK, BLK * BLK), 0.125, 0.75, ((0, 4), (1, 8))),
        "tile_ids": draw_tile_ids(jax.random.fold_in(keys[4], 71), 0),
        "occ_blocks": normal_values(keys[2], (NB, BLK * BLK), BLK ** -0.5, 0.75, ((0, 8),)),
        "virt_blocks": normal_values(keys[3], (NB, 2, BLK * BLK), BLK ** -0.5, 0.75, ((0, 8),)),
    }


def green_three(virt_blocks, col_block):
    zero_row = jnp.zeros_like(virt_blocks[0, 0])
    virt_diag = virt_blocks[col_block, 0]
    virt_up = jnp.where((col_block + 1 < NB)[:, None], virt_blocks[col_block, 1], zero_row[None, :])
    prev_block = jnp.maximum(col_block - 1, 0)
    virt_down = jnp.where((col_block >= 1)[:, None], virt_blocks[prev_block, 1], zero_row[None, :])
    count = col_block.shape[0]
    virt_down = jnp.transpose(virt_down.reshape(count, BLK, BLK), (0, 2, 1))
    return jnp.stack([virt_down, virt_diag.reshape(count, BLK, BLK), virt_up.reshape(count, BLK, BLK)], axis=1)


def make_rows(tile_set, ids, occ_blocks, virt_blocks):
    count = tile_set.shape[0]
    occ_pick = occ_blocks[ids[1]].reshape(count, BLK, BLK).astype(jnp.float32)
    four_dim = tile_set.reshape(count, BLK, BLK, BLK).astype(jnp.float32)
    half_done = jnp.einsum('tmn,tPnv->tPmv', occ_pick, four_dim).astype(jnp.bfloat16)
    virt_set = green_three(virt_blocks, ids[2]).astype(jnp.float32)
    rows_out = jnp.einsum('tPmv,tjvs->tjPms', half_done.astype(jnp.float32), virt_set).astype(jnp.bfloat16)
    return rows_out.reshape(count, 3, BLK, BLK * BLK)


def pair_terms(rows_in, partner, ids_left, ids_right):
    products = jnp.einsum('tjPk,uQk->tjPuQ', rows_in.astype(jnp.float32), partner.astype(jnp.float32))
    offsets = jnp.arange(3, dtype=jnp.int32) - 1
    live_left = ids_left[3].astype(jnp.float32)
    live_right = ids_right[3].astype(jnp.float32)
    same_row = (ids_right[1][None, None, :] == ids_left[1][:, None, None])
    near_col = (ids_right[2][None, None, :] == ids_left[2][:, None, None] + offsets[None, :, None])
    matches = (same_row & near_col).astype(jnp.float32) * live_left[:, None, None] * live_right[None, None, :]
    blocks_range = jnp.arange(RIB, dtype=jnp.int32)
    left_hot = (ids_left[0][:, None] == blocks_range[None, :]).astype(jnp.float32)
    right_hot = (ids_right[0][:, None] == blocks_range[None, :]).astype(jnp.float32)
    result = jnp.einsum('tp,tju,tjPuQ,uq->pPqQ', left_hot, matches, products, right_hot)
    return result.reshape(RIB * BLK, RIB * BLK)


def reference(tiles, tile_ids, occ_blocks, virt_blocks):
    zero_index = jnp.zeros((), jnp.int32)

    def device_terms(index):
        group_index = (index // N_MEM).astype(jnp.int32)
        mem_index = (index % N_MEM).astype(jnp.int32)
        low_group = jnp.maximum(group_index - 1, 0).astype(jnp.int32)
        column = (mem_index * SLOTS).astype(jnp.int32)
        mine_tiles = lax.dynamic_slice(tiles, (group_index, column, zero_index, zero_index), (1, SLOTS, BLK, BLK * BLK))[0]
        below_tiles = lax.dynamic_slice(tiles, (low_group, column, zero_index, zero_index), (1, SLOTS, BLK, BLK * BLK))[0]
        ids_own = lax.dynamic_slice(tile_ids, (group_index, zero_index, column), (1, 4, SLOTS))[0]
        ids_low = lax.dynamic_slice(tile_ids, (low_group, zero_index, column), (1, 4, SLOTS))[0]
        ids_low = ids_low.at[3].multiply((group_index > 0).astype(jnp.int32))
        rows_own = make_rows(mine_tiles, ids_own, occ_blocks, virt_blocks)
        return pair_terms(rows_own, mine_tiles, ids_own, ids_own), pair_terms(rows_own, below_tiles, ids_own, ids_low)

    middle_parts, lower_parts = lax.map(device_terms, jnp.arange(N_GRP * N_MEM, dtype=jnp.int32))
    group_rows = RIB * BLK
    middle = middle_parts.reshape(N_GRP, N_MEM, group_rows, group_rows).sum(axis=1)
    lower = lower_parts.reshape(N_GRP, N_MEM, group_rows, group_rows).sum(axis=1)
    upper = jnp.concatenate([jnp.transpose(lower[1:], (0, 2, 1)), jnp.zeros((1, group_rows, group_rows), jnp.float32)], axis=0)
    band = jnp.concatenate([lower, middle, upper], axis=2)
    return band.reshape(N_GRP * group_rows, 3 * group_rows)
```

```python
import functools
import math

import jax
import jax.numpy as jnp
from jax import lax
from jax.experimental import pallas as pl
from jax.experimental.pallas import tpu as pltpu
from jax.sharding import PartitionSpec as P

RIB = 4
WIDE = 256
HIGH = lax.Precision.HIGHEST
F32 = jnp.float32
BF16 = jnp.bfloat16
VMEM_BYTES = 48 * 1024 * 1024


def is_odd():
    return lax.rem(lax.axis_index("grp"), 2) == 1


def half_kernel(rows, ids, occ, tiles, half, even, odd, rows_in, rows_out, spread, made):
    side, flat = tiles.shape[2], tiles.shape[3]
    lanes = 2 * side
    high = flat // lanes
    cut = even.shape[2]
    slot = pl.program_id(0)
    group = lax.axis_index("grp")
    first = lax.axis_index("mem") * rows
    end = (ids[group, 1, slot] != first).astype(jnp.int32)
    low = lax.broadcasted_iota(jnp.int32, (high, lanes), 1) < side
    for h in range(high):
        rows_in[h * side : (h + 1) * side, :] = tiles[0, 0, :, h * lanes : (h + 1) * lanes].astype(F32)
    for p in range(0, side, 2):
        one = rows_in[pl.ds(p, high, stride=side), :]
        two = rows_in[pl.ds(p + 1, high, stride=side), :]
        at = slice(p * side, (p + 2) * side)
        spread[:high, at] = jnp.where(low, one, pltpu.roll(two, side, 1)).astype(BF16)
        spread[high:, at] = jnp.where(low, pltpu.roll(one, side, 1), two).astype(BF16)
    made[...] = jnp.dot(occ[end], spread[...], preferred_element_type=F32)
    for p in range(0, side, 2):
        at = slice(p * side, (p + 2) * side)
        top, bottom = made[:high, at], made[high:, at]
        rows_out[pl.ds(p, high, stride=side), :] = jnp.where(low, top, pltpu.roll(bottom, side, 1))
        rows_out[pl.ds(p + 1, high, stride=side), :] = jnp.where(low, pltpu.roll(top, side, 1), bottom)
    for h in range(high):
        half[0, :, h * lanes : (h + 1) * lanes] = rows_out[h * side : (h + 1) * side, :].astype(BF16)

    @pl.when(is_odd())
    def _():
        even[0] = half[0, :, cut:]
        odd[0] = tiles[0, 0, :, :cut]

    @pl.when(jnp.logical_not(is_odd()))
    def _():
        even[0] = tiles[0, 0, :, :cut]
        odd[0] = half[0, :, cut:]


def combined(products, slots, side, ids, left, right, left_on, right_on, total):
    width = slots * side
    owner = lax.broadcasted_iota(jnp.int32, (1, width), 1) // side
    total[...] = jnp.zeros_like(total)
    for t in range(slots):
        term = jnp.zeros((side, width), F32)
        for j in range(3):
            mask = jnp.zeros((1, width), F32)
            for u in range(slots):
                same = (
                    (ids[left, 1, t] == ids[right, 1, u])
                    & (ids[right, 2, u] == ids[left, 2, t] + (j - 1))
                    & (ids[left, 3, t] * left_on * ids[right, 3, u] * right_on > 0)
                )
                mask = jnp.where(owner == u, same.astype(F32), mask)
            at = (t * 3 + j) * side
            term = term + products[at : at + side, :] * mask
        total[ids[left, 0, t]] += term
    row = lax.broadcasted_iota(jnp.int32, (width, RIB * side), 0)
    column = lax.broadcasted_iota(jnp.int32, (width, RIB * side), 1)
    target = jnp.zeros((width, RIB * side), jnp.int32)
    for u in range(slots):
        target = jnp.where(row // side == u, ids[right, 0, u] * side + lax.rem(row, side), target)
    place = (target == column).astype(F32)
    return jnp.dot(total[...].reshape(RIB * side, width), place, precision=HIGH, preferred_element_type=F32)


NT = (((1,), (1,)), ((), ()))
NN = (((1,), (0,)), ((), ()))


def prepare_kernel(rows, ids, half, tiles, table, y_low, v_high, middle, y_all, total):
    slots, side, flat = half.shape
    cut = y_low.shape[1]
    group = lax.axis_index("grp")
    first = lax.axis_index("mem") * rows
    count = rows * lax.axis_size("mem")
    copies = WIDE // side
    own = lax.broadcasted_iota(jnp.int32, (WIDE, WIDE), 0) // side
    own = own == lax.broadcasted_iota(jnp.int32, (WIDE, WIDE), 1) // side

    def spread(block):
        row = jnp.concatenate([block] * copies, axis=1)
        return jnp.where(own, jnp.concatenate([row] * copies, axis=0), jnp.zeros((), BF16))

    for t in range(slots):
        a, b = ids[group, 1, t], ids[group, 2, t]
        at = jnp.where(a == first, 2, 6) + b - a
        keep = (b + 1 < count).astype(F32)
        before = spread(table[at - 1, 1])
        here = spread(table[at, 0])
        after = spread((table[at, 1].astype(F32) * keep).astype(BF16))
        x = jnp.concatenate([half[t, :, c : c + WIDE] for c in range(0, flat, WIDE)], axis=0)
        for j, (mat, dims) in enumerate(((before, NT), (here, NN), (after, NN))):
            y = lax.dot_general(x, mat, dims, preferred_element_type=F32).astype(BF16)
            for c in range(0, flat, WIDE):
                block = y[c // WIDE * side : (c // WIDE + 1) * side]
                y_all[(t * 3 + j) * side : (t * 3 + j + 1) * side, c : c + WIDE] = block
                if c < cut:
                    y_low[(t * 3 + j) * side : (t * 3 + j + 1) * side, c : c + WIDE] = block
        x = jnp.concatenate([tiles[0, t, :, c : c + WIDE] for c in range(cut, flat, WIDE)], axis=0)
        for j, (mat, dims) in enumerate(((before, NT), (here, NT), (after, NN))):
            y = lax.dot_general(x, mat, dims, preferred_element_type=F32).astype(BF16)
            for c in range(0, flat - cut, WIDE):
                block = y[c // WIDE * side : (c // WIDE + 1) * side]
                v_high[(t * 3 + j) * side : (t * 3 + j + 1) * side, c : c + WIDE] = block
    products = lax.dot_general(
        y_all[...], tiles[0].reshape(slots * side, flat), NT, preferred_element_type=F32
    )
    middle[...] = combined(products, slots, side, ids, group, group, 1, 1, total)


def pair_kernel(ids, y_low, v_high, even, odd, lower, upper, out_even, out_odd, below, above, total, sem):
    slots, side, _ = even.shape
    group = lax.axis_index("grp")
    last = lax.axis_size("grp") - 1
    has_below = (group > 0).astype(jnp.int32)
    has_above = (group < last).astype(jnp.int32)
    under, over = jnp.maximum(group - 1, 0), jnp.minimum(group + 1, last)

    @pl.when(is_odd())
    def _():
        pltpu.make_async_copy(even, below, sem.at[0]).start()
        pltpu.make_async_copy(odd, above, sem.at[1]).start()

    @pl.when(jnp.logical_not(is_odd()))
    def _():
        pltpu.make_async_copy(odd, below, sem.at[0]).start()
        pltpu.make_async_copy(even, above, sem.at[1]).start()

    pltpu.make_async_copy(even, below, sem.at[0]).wait()
    products = lax.dot_general(
        y_low[...], below[...].reshape(slots * side, -1), NT, preferred_element_type=F32
    )
    lower[...] = combined(products, slots, side, ids, group, under, 1, has_below, total)
    pltpu.make_async_copy(odd, above, sem.at[1]).wait()
    products = lax.dot_general(
        v_high[...], above[...].reshape(slots * side, -1), NT, preferred_element_type=F32
    )
    upper[...] = combined(products, slots, side, ids, group, over, 1, has_above, total)
    to_below = lower[...].T.astype(BF16)
    to_above = upper[...].T.astype(BF16)
    odd_one = is_odd()
    out_even[...] = jnp.where(odd_one, to_below, to_above)
    out_odd[...] = jnp.where(odd_one, to_above, to_below)


def band_kernel(lower, middle, upper, even, odd, band):
    side = lower.shape[1]
    odd_one = is_odd()
    from_even, from_odd = even[...].astype(F32), odd[...].astype(F32)
    band[:, :side] = (lower[...] + jnp.where(odd_one, from_even, from_odd)).astype(BF16)
    band[:, side : 2 * side] = middle[...].astype(BF16)
    band[:, 2 * side :] = (upper[...] + jnp.where(odd_one, from_odd, from_even)).astype(BF16)


def swapped(block, parity):
    count = lax.axis_size("grp")
    pairs = [(i, i + 1) for i in range(parity, count - 1, 2)]
    return lax.ppermute(block, "grp", pairs + [(b, a) for a, b in pairs])


def params(**more):
    return pltpu.CompilerParams(vmem_limit_bytes=VMEM_BYTES, **more)


WHOLE = pl.BlockSpec(memory_space=pltpu.VMEM)
SCALAR = pl.BlockSpec(memory_space=pltpu.SMEM)


def body(tiles, tile_ids, occ_blocks, virt_blocks):
    slots, side, flat = tiles.shape[1:]
    rows = occ_blocks.shape[0]
    members = lax.axis_size("mem")
    cut = flat // 2
    width = RIB * side

    ends = jnp.concatenate([occ_blocks[:1], occ_blocks[rows - 1 :]], axis=0)
    ends = ends.reshape(2, side // 2, 2, side // 2, 2).transpose(0, 2, 1, 4, 3).reshape(2, side, side)
    one_slot = lambda lanes: pl.BlockSpec((1, side, lanes), lambda i: (i, 0, 0))
    half, even, odd = pl.pallas_call(
        functools.partial(half_kernel, rows),
        grid=(slots,),
        in_specs=[SCALAR, WHOLE, pl.BlockSpec((1, 1, side, flat), lambda i: (0, i, 0, 0))],
        out_specs=[one_slot(flat), one_slot(cut), one_slot(cut)],
        out_shape=[
            jax.ShapeDtypeStruct((slots, side, flat), BF16),
            jax.ShapeDtypeStruct((slots, side, cut), BF16),
            jax.ShapeDtypeStruct((slots, side, cut), BF16),
        ],
        scratch_shapes=[
            pltpu.VMEM((flat // 2, 2 * side), F32),
            pltpu.VMEM((flat // 2, 2 * side), F32),
            pltpu.VMEM((side, flat), BF16),
            pltpu.VMEM((side, flat), F32),
        ],
        compiler_params=params(),
    )(tile_ids, ends, tiles)
    got_odd = swapped(odd, 1)
    got_even = swapped(even, 0)

    forward = [(i, i + 1) for i in range(members - 1)]
    backward = [(b, a) for a, b in forward]
    before = lax.ppermute(virt_blocks[rows - 2 :], "mem", forward)
    after = lax.ppermute(virt_blocks[:1], "mem", backward)
    table = jnp.concatenate([before, virt_blocks[:2], virt_blocks[rows - 3 :], after], axis=0)
    table = table.reshape(8, 2, side, side)

    ids = tile_ids
    y_low, v_high, middle = pl.pallas_call(
        functools.partial(prepare_kernel, rows),
        in_specs=[SCALAR, WHOLE, WHOLE, WHOLE],
        out_specs=[WHOLE, WHOLE, WHOLE],
        out_shape=[
            jax.ShapeDtypeStruct((slots * 3 * side, cut), BF16),
            jax.ShapeDtypeStruct((slots * 3 * side, flat - cut), BF16),
            jax.ShapeDtypeStruct((width, width), F32),
        ],
        scratch_shapes=[
            pltpu.VMEM((slots * 3 * side, flat), BF16),
            pltpu.VMEM((RIB, side, slots * side), F32),
        ],
        compiler_params=params(),
    )(ids, half, tiles, table)
    lower, upper, out_even, out_odd = pl.pallas_call(
        pair_kernel,
        in_specs=[SCALAR, WHOLE, WHOLE, pl.BlockSpec(memory_space=pl.ANY), pl.BlockSpec(memory_space=pl.ANY)],
        out_specs=[WHOLE] * 4,
        out_shape=[jax.ShapeDtypeStruct((width, width), F32)] * 2
        + [jax.ShapeDtypeStruct((width, width), BF16)] * 2,
        scratch_shapes=[
            pltpu.VMEM((slots, side, cut), BF16),
            pltpu.VMEM((slots, side, cut), BF16),
            pltpu.VMEM((RIB, side, slots * side), F32),
            pltpu.SemaphoreType.DMA((2,)),
        ],
        compiler_params=params(),
    )(ids, y_low, v_high, got_even, got_odd)
    back_odd = swapped(out_odd, 1)
    back_even = swapped(out_even, 0)
    band = pl.pallas_call(
        band_kernel,
        in_specs=[WHOLE] * 5,
        out_specs=WHOLE,
        out_shape=jax.ShapeDtypeStruct((width, 3 * width), BF16),
        compiler_params=params(),
    )(lower, middle, upper, back_even, back_odd)
    parts = lax.all_to_all(band.reshape(members, width // members, 3 * width), "mem", 0, 0)
    return parts.astype(F32).sum(axis=0)


def solution(mesh):
    placed = (
        P("grp", "mem", None, None),
        P(None, None, "mem"),
        P("mem", None),
        P("mem", None, None),
    )
    return jax.shard_map(
        body, mesh=mesh, in_specs=placed, out_specs=P(("grp", "mem"), None), check_vma=False
    )
```

```python
import functools

import jax
import jax.numpy as jnp
from jax import lax
from jax.experimental import pallas as pl
from jax.experimental.pallas import tpu as pltpu
from jax.sharding import PartitionSpec as P

RIB = 4
WIDE = 256
F32 = jnp.float32
BF16 = jnp.bfloat16


def is_odd():
    return lax.rem(lax.axis_index("grp"), 2) == 1


def half_kernel(
    occ_in, ids_in, tiles, virt, half, even, odd, send_up, send_down, held, made, to_even, to_odd,
    occ, ids, green, rows_in, rows_out, sem, out_sem
):
    slots, side, flat = held.shape
    lanes, cut = 2 * side, even.shape[2]
    high = flat // lanes
    pitch = rows_in.shape[0] // high
    rows = occ.shape[0]
    first_in = pltpu.make_async_copy(occ_in, occ, sem.at[slots + 2])
    ids_copy = pltpu.make_async_copy(ids_in, ids, sem.at[slots + 3])
    first_in.start()
    ids_copy.start()
    fetch = [pltpu.make_async_copy(tiles.at[0, t], held.at[t], sem.at[t]) for t in range(slots)]
    for copy in fetch:
        copy.start()
    up = pltpu.make_async_copy(virt.at[pl.ds(rows - 2, 2)], send_up, sem.at[slots])
    down = pltpu.make_async_copy(virt.at[pl.ds(0, 1)], send_down, sem.at[slots + 1])
    up.start()
    down.start()
    group = lax.axis_index("grp")
    first = lax.axis_index("mem") * rows
    odd_one = is_odd()
    source = lax.broadcasted_iota(jnp.int32, (lanes, side), 0)
    target = lax.broadcasted_iota(jnp.int32, (lanes, side), 1)
    mu = lax.rem(source, side)
    first_in.wait()
    for end, row in enumerate((0, rows - 1)):
        line = occ[row : row + 1, :].astype(F32)
        block = jnp.concatenate([line[:, h * lanes : (h + 1) * lanes] for h in range(high)], axis=0)
        for parity in range(2):
            other = (lax.rem(mu, 2) != parity).astype(jnp.int32)
            pick = (source // side == parity) & (target == mu // 2 + other * high)
            green[end, parity * high : (parity + 1) * high, :] = jnp.dot(
                block.astype(BF16), pick.astype(BF16), preferred_element_type=F32
            ).astype(BF16)
    low = lax.broadcasted_iota(jnp.int32, (high, lanes), 1) < side
    ids_copy.wait()
    results = []
    for t in range(slots):
        fetch[t].wait()
        block = green[(ids[group, 1, t] != first).astype(jnp.int32)]
        for h in range(high):
            rows_in[h * pitch : h * pitch + side, :] = held[t, :, h * lanes : (h + 1) * lanes].astype(F32)
        for p in range(0, side, 2):
            one = rows_in[pl.ds(p, high, stride=pitch), :]
            two = rows_in[pl.ds(p + 1, high, stride=pitch), :]
            crossed = [pltpu.roll(one, side, 1), pltpu.roll(two, side, 1)]
            x = jnp.concatenate(
                [jnp.concatenate([one, two], axis=1), jnp.concatenate(crossed, axis=1)], axis=0
            )
            y = jnp.dot(block, x.astype(BF16), preferred_element_type=F32)
            rows_out[pl.ds(p, high, stride=pitch), :] = jnp.where(low, y[:high, :lanes], y[high:, :lanes])
            rows_out[pl.ds(p + 1, high, stride=pitch), :] = jnp.where(low, y[:high, lanes:], y[high:, lanes:])
        for h in range(high):
            at = slice(h * lanes, (h + 1) * lanes)
            done = rows_out[h * pitch : h * pitch + side, :].astype(BF16)
            made[t, :, at] = done
            if h * lanes >= cut:
                raw = held[t, :, h * lanes - cut : (h + 1) * lanes - cut]
                to = slice(h * lanes - cut, (h + 1) * lanes - cut)
                to_even[t, :, to] = jnp.where(odd_one, done, raw)
                to_odd[t, :, to] = jnp.where(odd_one, raw, done)
        for k, (source, target) in enumerate(((to_even, even), (to_odd, odd), (made, half))):
            copy = pltpu.make_async_copy(source.at[t], target.at[t], out_sem.at[t, k])
            copy.start()
            results.append(copy)
    for copy in results + [up, down]:
        copy.wait()


def combined(products, slots, side, ids, left, right, left_on, right_on, total):
    width = slots * side

    def spread(values, owner):
        out = jnp.full(owner.shape, values[0], jnp.int32)
        for u in range(1, slots):
            out = jnp.where(owner == u, values[u], out)
        return out

    owner = lax.broadcasted_iota(jnp.int32, (1, width), 1) // side
    live = [ids[right, 3, u] * right_on for u in range(slots)]
    row_block = spread([jnp.where(live[u] > 0, ids[right, 1, u], -1) for u in range(slots)], owner)
    col_block = spread([ids[right, 2, u] for u in range(slots)], owner)
    total[...] = jnp.zeros_like(total)
    for t in range(slots):
        same = row_block == jnp.where(ids[left, 3, t] * left_on > 0, ids[left, 1, t], -2)
        term = jnp.zeros((side, width), F32)
        for j in range(3):
            at = (t * 3 + j) * side
            match = (same & (col_block == ids[left, 2, t] + (j - 1))).astype(F32)
            term = term + products[at : at + side, :] * match
        total[ids[left, 0, t]] += term
    row = lax.broadcasted_iota(jnp.int32, (width, 1), 0)
    target = spread([ids[right, 0, u] for u in range(slots)], row // side) * side + lax.rem(row, side)
    place = (target == lax.broadcasted_iota(jnp.int32, (width, RIB * side), 1)).astype(F32).astype(BF16)
    summed = total[...].reshape(RIB * side, width)
    coarse = summed.astype(BF16)
    fine = (summed - coarse.astype(F32)).astype(BF16)
    return jnp.dot(coarse, place, preferred_element_type=F32) + jnp.dot(
        fine, place, preferred_element_type=F32
    )


NT = (((1,), (1,)), ((), ()))
NN = (((1,), (0,)), ((), ()))


def prepare_kernel(rows, ids, half, tiles, table, y_all, v_high, middle, total, products):
    slots, side, flat = half.shape
    cut = flat - v_high.shape[1]
    group = lax.axis_index("grp")
    first = lax.axis_index("mem") * rows
    count = rows * lax.axis_size("mem")
    copies = WIDE // side
    own = lax.broadcasted_iota(jnp.int32, (WIDE, WIDE), 0) // side
    own = own == lax.broadcasted_iota(jnp.int32, (WIDE, WIDE), 1) // side

    def spread(block):
        row = jnp.concatenate([block] * copies, axis=1)
        return jnp.where(own, jnp.concatenate([row] * copies, axis=0), jnp.zeros((), BF16))

    for t in range(slots):
        a, b = ids[group, 1, t], ids[group, 2, t]
        at = jnp.where(a == first, 2, 6) + b - a
        keep = (b + 1 < count).astype(F32)
        before = spread(table[at - 1, 1])
        here = spread(table[at, 0])
        after = spread((table[at, 1].astype(F32) * keep).astype(BF16))
        x = jnp.concatenate([half[t, :, c : c + WIDE] for c in range(0, flat, WIDE)], axis=0)
        for j, (mat, dims) in enumerate(((before, NT), (here, NN), (after, NN))):
            y = lax.dot_general(x, mat, dims, preferred_element_type=F32).astype(BF16)
            for c in range(0, flat, WIDE):
                block = y[c // WIDE * side : (c // WIDE + 1) * side]
                y_all[(t * 3 + j) * side : (t * 3 + j + 1) * side, c : c + WIDE] = block
        x = jnp.concatenate([tiles[0, t, :, c : c + WIDE] for c in range(cut, flat, WIDE)], axis=0)
        for j, (mat, dims) in enumerate(((before, NT), (here, NT), (after, NN))):
            y = lax.dot_general(x, mat, dims, preferred_element_type=F32).astype(BF16)
            for c in range(0, flat - cut, WIDE):
                block = y[c // WIDE * side : (c // WIDE + 1) * side]
                v_high[(t * 3 + j) * side : (t * 3 + j + 1) * side, c : c + WIDE] = block
    products[...] = lax.dot_general(
        y_all[...], tiles[0].reshape(slots * side, flat), NT, preferred_element_type=F32
    )
    middle[...] = combined(products, slots, side, ids, group, group, 1, 1, total)


def pair_kernel(ids, y_all, v_high, even, odd, lower, upper, out_even, out_odd, total, products):
    slots, side, _ = even.shape
    group = lax.axis_index("grp")
    last = lax.axis_size("grp") - 1
    has_below = (group > 0).astype(jnp.int32)
    has_above = (group < last).astype(jnp.int32)
    under, over = jnp.maximum(group - 1, 0), jnp.minimum(group + 1, last)

    odd_one = is_odd()
    cut = even.shape[2]
    from_even = even[...].reshape(slots * side, cut)
    from_odd = odd[...].reshape(slots * side, cut)
    products[...] = lax.dot_general(
        y_all[:, :cut], jnp.where(odd_one, from_even, from_odd), NT, preferred_element_type=F32
    )
    lower[...] = combined(products, slots, side, ids, group, under, 1, has_below, total)
    products[...] = lax.dot_general(
        v_high[...], jnp.where(odd_one, from_odd, from_even), NT, preferred_element_type=F32
    )
    upper[...] = combined(products, slots, side, ids, group, over, 1, has_above, total)
    to_below = lower[...].T.astype(BF16)
    to_above = upper[...].T.astype(BF16)
    out_even[...] = jnp.where(odd_one, to_below, to_above)
    out_odd[...] = jnp.where(odd_one, to_above, to_below)


def band_kernel(lower, middle, upper, even, odd, band):
    side = lower.shape[1]
    odd_one = is_odd()
    from_even, from_odd = even[...].astype(F32), odd[...].astype(F32)
    band[:, :side] = (lower[...] + jnp.where(odd_one, from_even, from_odd)).astype(BF16)
    band[:, side : 2 * side] = middle[...].astype(BF16)
    band[:, 2 * side :] = (upper[...] + jnp.where(odd_one, from_odd, from_even)).astype(BF16)


def swapped(block, parity):
    count = lax.axis_size("grp")
    pairs = [(i, i + 1) for i in range(parity, count - 1, 2)]
    return lax.ppermute(block, "grp", pairs + [(b, a) for a, b in pairs])


def params(mib):
    return pltpu.CompilerParams(vmem_limit_bytes=mib * 1024 * 1024)


def in_hbm(x):
    return pltpu.with_memory_space_constraint(x, pltpu.HBM)


def in_vmem(x):
    return pltpu.with_memory_space_constraint(x, pltpu.VMEM)


WHOLE = pl.BlockSpec(memory_space=pltpu.VMEM)
SCALAR = pl.BlockSpec(memory_space=pltpu.SMEM)


def body(tiles, tile_ids, occ_blocks, virt_blocks):
    slots, side, flat = tiles.shape[1:]
    rows = occ_blocks.shape[0]
    members = lax.axis_size("mem")
    cut = flat // 2
    width = RIB * side

    anywhere = pl.BlockSpec(memory_space=pltpu.HBM)
    pitch = side + 8
    half, even, odd, send_up, send_down = pl.pallas_call(
        half_kernel,
        in_specs=[anywhere] * 4,
        out_specs=[anywhere] * 5,
        out_shape=[
            pltpu.HBM((slots, side, flat), BF16),
            pltpu.HBM((slots, side, cut), BF16),
            pltpu.HBM((slots, side, cut), BF16),
            jax.ShapeDtypeStruct((2, 2, flat), BF16),
            jax.ShapeDtypeStruct((1, 2, flat), BF16),
        ],
        scratch_shapes=[
            pltpu.VMEM((slots, side, flat), BF16),
            pltpu.VMEM((slots, side, flat), BF16),
            pltpu.VMEM((slots, side, cut), BF16),
            pltpu.VMEM((slots, side, cut), BF16),
            pltpu.VMEM(occ_blocks.shape, BF16),
            pltpu.SMEM(tile_ids.shape, jnp.int32),
            pltpu.VMEM((2, side, side), BF16),
            pltpu.VMEM((flat // (2 * side) * pitch, 2 * side), F32),
            pltpu.VMEM((flat // (2 * side) * pitch, 2 * side), F32),
            pltpu.SemaphoreType.DMA((slots + 4,)),
            pltpu.SemaphoreType.DMA((slots, 3)),
        ],
        compiler_params=params(16),
    )(*(in_hbm(x) for x in (occ_blocks, tile_ids, tiles, virt_blocks)))
    got_odd = swapped(odd, 1)
    got_even = swapped(even, 0)

    forward = [(i, i + 1) for i in range(members - 1)]
    backward = [(b, a) for a, b in forward]
    before = lax.ppermute(send_up, "mem", forward)
    after = lax.ppermute(send_down, "mem", backward)
    table = jnp.concatenate([before, virt_blocks[:2], virt_blocks[rows - 3 :], after], axis=0)
    table = table.reshape(8, 2, side, side)

    y_all, v_high, middle = pl.pallas_call(
        functools.partial(prepare_kernel, rows),
        in_specs=[SCALAR, WHOLE, WHOLE, WHOLE],
        out_specs=[WHOLE, WHOLE, WHOLE],
        out_shape=[
            pltpu.VMEM((slots * 3 * side, flat), BF16),
            pltpu.VMEM((slots * 3 * side, flat - cut), BF16),
            pltpu.VMEM((width, width), F32),
        ],
        scratch_shapes=[pltpu.VMEM((RIB, side, slots * side), F32),
            pltpu.VMEM((slots * 3 * side, slots * side), F32),
        ],
        compiler_params=params(24),
    )(tile_ids, half, tiles, table)
    lower, upper, out_even, out_odd = pl.pallas_call(
        pair_kernel,
        in_specs=[SCALAR] + [WHOLE] * 4,
        out_specs=[WHOLE] * 4,
        out_shape=[jax.ShapeDtypeStruct((width, width), F32)] * 2
        + [jax.ShapeDtypeStruct((width, width), BF16)] * 2,
        scratch_shapes=[pltpu.VMEM((RIB, side, slots * side), F32),
            pltpu.VMEM((slots * 3 * side, slots * side), F32),
        ],
        compiler_params=params(24),
    )(tile_ids, in_vmem(y_all), in_vmem(v_high), in_vmem(got_even), in_vmem(got_odd))
    back_odd = swapped(out_odd, 1)
    back_even = swapped(out_even, 0)
    band = pl.pallas_call(
        band_kernel,
        in_specs=[WHOLE] * 5,
        out_specs=WHOLE,
        out_shape=jax.ShapeDtypeStruct((width, 3 * width), BF16),
        compiler_params=params(8),
    )(lower, middle, upper, back_even, back_odd)
    parts = lax.all_to_all(band.reshape(members, width // members, 3 * width), "mem", 0, 0)
    return parts.astype(F32).sum(axis=0)


def solution(mesh):
    placed = (
        P("grp", "mem", None, None),
        P(None, None, "mem"),
        P("mem", None),
        P("mem", None, None),
    )
    return jax.shard_map(
        body, mesh=mesh, in_specs=placed, out_specs=P(("grp", "mem"), None), check_vma=False
    )
```

```python
import functools

import jax
import jax.numpy as jnp
from jax import lax
from jax.experimental import pallas as pl
from jax.experimental.pallas import tpu as pltpu
from jax.sharding import PartitionSpec as P

RIB = 4
WIDE = 256
F32 = jnp.float32
BF16 = jnp.bfloat16


def is_odd():
    return lax.rem(lax.axis_index("grp"), 2) == 1


def go_rows(block, source, rows_in, rows_out, result):
    side = source.shape[0]
    lanes = 2 * side
    high = source.shape[1] // lanes
    some = block.shape[0] // 2
    pitch = rows_in.shape[0] // high
    low = lax.broadcasted_iota(jnp.int32, (some, lanes), 1) < side
    for h in range(high):
        rows_in[h * pitch : h * pitch + side, :] = source[:, h * lanes : (h + 1) * lanes].astype(F32)
    for p in range(0, side, 2):
        one = rows_in[pl.ds(p, high, stride=pitch), :]
        two = rows_in[pl.ds(p + 1, high, stride=pitch), :]
        crossed = [pltpu.roll(one, side, 1), pltpu.roll(two, side, 1)]
        x = jnp.concatenate(
            [jnp.concatenate([one, two], axis=1), jnp.concatenate(crossed, axis=1)], axis=0
        )
        y = jnp.dot(block, x.astype(BF16), preferred_element_type=F32)
        rows_out[pl.ds(p, some, stride=pitch), :] = jnp.where(low, y[:some, :lanes], y[some:, :lanes])
        rows_out[pl.ds(p + 1, some, stride=pitch), :] = jnp.where(low, y[:some, lanes:], y[some:, lanes:])
    for h in range(some):
        result(slice(h * lanes, (h + 1) * lanes), rows_out[h * pitch : h * pitch + side, :].astype(BF16))


def send_kernel(
    occ_in, ids_in, tiles, virt, even, odd, send_up, send_down, near, far, green, held, to_even, to_odd,
    occ, ids, rows_in, rows_out, sem, out_sem
):
    slots, side, flat = held.shape
    lanes, cut = 2 * side, even.shape[2]
    high = flat // lanes
    rows = occ.shape[0]
    first_in = pltpu.make_async_copy(occ_in, occ, sem.at[slots + 2])
    ids_copy = pltpu.make_async_copy(ids_in, ids, sem.at[slots + 3])
    first_in.start()
    ids_copy.start()
    fetch = [pltpu.make_async_copy(tiles.at[0, t], held.at[t], sem.at[t]) for t in range(slots)]
    for copy in fetch:
        copy.start()
    up = pltpu.make_async_copy(virt.at[pl.ds(rows - 2, 2)], send_up, sem.at[slots])
    down = pltpu.make_async_copy(virt.at[pl.ds(0, 1)], send_down, sem.at[slots + 1])
    near_copy = pltpu.make_async_copy(virt.at[pl.ds(0, 2)], near, sem.at[slots + 4])
    far_copy = pltpu.make_async_copy(virt.at[pl.ds(rows - 3, 3)], far, sem.at[slots + 5])
    edges = [up, down, near_copy, far_copy]
    for copy in edges:
        copy.start()
    group = lax.axis_index("grp")
    first = lax.axis_index("mem") * rows
    odd_one = is_odd()
    source = lax.broadcasted_iota(jnp.int32, (lanes, side), 0)
    target = lax.broadcasted_iota(jnp.int32, (lanes, side), 1)
    mu = lax.rem(source, side)
    some = high // 2
    first_in.wait()
    for end, row in enumerate((0, rows - 1)):
        line = occ[row : row + 1, :].astype(F32)
        block = jnp.concatenate([line[:, h * lanes : (h + 1) * lanes] for h in range(high)], axis=0)
        for parity in range(2):
            other = (lax.rem(mu, 2) != parity).astype(jnp.int32)
            pick = (source // side == parity) & (target == mu // 2 + other * high)
            chosen = jnp.dot(
                block.astype(BF16), pick.astype(BF16), preferred_element_type=F32
            ).astype(BF16)
            for part in range(2):
                green[end, part, parity * some : (parity + 1) * some, :] = chosen[part * some : (part + 1) * some]
    ids_copy.wait()
    results = []
    for t in range(slots):
        fetch[t].wait()
        block = green[(ids[group, 1, t] != first).astype(jnp.int32), 1]

        def result(at, done):
            raw = held[t, :, at]
            to_even[t, :, at] = jnp.where(odd_one, done, raw)
            to_odd[t, :, at] = jnp.where(odd_one, raw, done)

        go_rows(block, held.at[t], rows_in, rows_out, result)
        for k, (source, target) in enumerate(((to_odd, odd), (to_even, even))):
            copy = pltpu.make_async_copy(source.at[t], target.at[t], out_sem.at[t, k])
            copy.start()
            results.append(copy)
    for copy in results + edges:
        copy.wait()


def half_kernel(rows, ids, green, tiles, even, odd, half, rows_in, rows_out, sem):
    slots, side, flat = half.shape
    cut = even.shape[2]
    group = lax.axis_index("grp")
    first = lax.axis_index("mem") * rows
    high_part = half.at[:, :, pl.ds(cut, flat - cut)]

    @pl.when(is_odd())
    def _():
        pltpu.make_async_copy(even, high_part, sem.at[0]).start()

    @pl.when(jnp.logical_not(is_odd()))
    def _():
        pltpu.make_async_copy(odd, high_part, sem.at[0]).start()

    for t in range(slots):
        block = green[(ids[group, 1, t] != first).astype(jnp.int32), 0]

        def result(at, done):
            half[t, :, at] = done

        go_rows(block, tiles.at[0, t], rows_in, rows_out, result)
    pltpu.make_async_copy(even, high_part, sem.at[0]).wait()


def combined(products, slots, side, ids, left, right, left_on, right_on, total):
    width = slots * side

    def spread(values, owner):
        out = jnp.full(owner.shape, values[0], jnp.int32)
        for u in range(1, slots):
            out = jnp.where(owner == u, values[u], out)
        return out

    owner = lax.broadcasted_iota(jnp.int32, (1, width), 1) // side
    live = [ids[right, 3, u] * right_on for u in range(slots)]
    row_block = spread([jnp.where(live[u] > 0, ids[right, 1, u], -1) for u in range(slots)], owner)
    col_block = spread([ids[right, 2, u] for u in range(slots)], owner)
    total[...] = jnp.zeros_like(total)
    for t in range(slots):
        same = row_block == jnp.where(ids[left, 3, t] * left_on > 0, ids[left, 1, t], -2)
        term = jnp.zeros((side, width), F32)
        for j in range(3):
            at = (t * 3 + j) * side
            match = (same & (col_block == ids[left, 2, t] + (j - 1))).astype(F32)
            term = term + products[at : at + side, :] * match
        total[ids[left, 0, t]] += term
    ahead = lax.broadcasted_iota(jnp.int32, (side, RIB * side), 1)
    ahead = ahead - lax.broadcasted_iota(jnp.int32, (side, RIB * side), 0)
    place = [(ahead == ids[right, 0, u] * side).astype(F32).astype(BF16) for u in range(slots)]
    place = jnp.concatenate(place, axis=0)
    summed = total[...].reshape(RIB * side, width)
    coarse = summed.astype(BF16)
    fine = (summed - coarse.astype(F32)).astype(BF16)
    return jnp.dot(coarse, place, preferred_element_type=F32) + jnp.dot(
        fine, place, preferred_element_type=F32
    )


NT = (((1,), (1,)), ((), ()))
NN = (((1,), (0,)), ((), ()))


def prepare_kernel(rows, ids, before, near, far, after, half, tiles, y_all, v_high, table, mats):
    slots, side, flat = half.shape
    cut = flat - v_high.shape[1]
    group = lax.axis_index("grp")
    first = lax.axis_index("mem") * rows
    count = rows * lax.axis_size("mem")
    copies = WIDE // side
    own = lax.broadcasted_iota(jnp.int32, (WIDE, WIDE), 0) // side
    own = own == lax.broadcasted_iota(jnp.int32, (WIDE, WIDE), 1) // side
    own = own.astype(F32).astype(BF16)

    at = 0
    for source in (before, near, far, after):
        for k in range(source.shape[0]):
            table[at : at + 2, :] = source[k].astype(F32)
            at += 2
    lanes = 2 * side
    pairs = side // 2
    line_of = lax.broadcasted_iota(jnp.int32, (side, pairs), 0) // 2
    line_of = (line_of == lax.broadcasted_iota(jnp.int32, (side, pairs), 1)).astype(F32).astype(BF16)
    even_row = lax.rem(lax.broadcasted_iota(jnp.int32, (side, lanes), 0), 2) == 0
    straight = even_row == (lax.broadcasted_iota(jnp.int32, (side, lanes), 1) < side)

    def spread(row, keep=None):
        line = table[pl.ds(row, 1), :]
        if keep is not None:
            line = line * keep
        block = jnp.concatenate([line[:, h * lanes : (h + 1) * lanes] for h in range(pairs)], axis=0)
        block = jnp.dot(line_of, block.astype(BF16), preferred_element_type=F32)
        block = jnp.where(straight, block, pltpu.roll(block, side, 1)).astype(BF16)
        row = jnp.concatenate([block] * (copies // 2), axis=1)
        return jnp.concatenate([row] * copies, axis=0) * own

    for t in range(slots):
        a, b = ids[group, 1, t], ids[group, 2, t]
        at = jnp.where(a == first, 2, 6) + b - a
        keep = (b + 1 < count).astype(F32)
        mats[t * 3] = spread(2 * at - 1)
        mats[t * 3 + 1] = spread(2 * at)
        mats[t * 3 + 2] = spread(2 * at + 1, keep)

    def transform(source, low, result, dims):
        lanes = result.shape[1]
        for t in range(slots):
            x = [source[t, :, c : c + WIDE] for c in range(low, low + lanes, WIDE)]
            x = jnp.concatenate(x, axis=0)
            for j in range(3):
                y = lax.dot_general(x, mats[t * 3 + j], dims[j], preferred_element_type=F32).astype(BF16)
                at = slice((t * 3 + j) * side, (t * 3 + j + 1) * side)
                for k in range(lanes // WIDE):
                    result[at, k * WIDE : (k + 1) * WIDE] = y[k * side : (k + 1) * side]

    transform(half, 0, y_all, (NT, NN, NN))
    transform(tiles.at[0], cut, v_high, (NT, NT, NN))


def middle_kernel(ids, y_all, tiles, after, middle, total, products):
    slots, side, flat = tiles.shape[1:]
    group = lax.axis_index("grp")
    products[...] = lax.dot_general(
        y_all[...], tiles[0].reshape(slots * side, flat), NT, preferred_element_type=F32
    )
    middle[...] = combined(products, slots, side, ids, group, group, 1, 1, total)


def pair_kernel(odd_is_upper_group, ids, y_all, v_high, other, part, send, total, products):
    slots, side, cut = other.shape
    group = lax.axis_index("grp")
    last = lax.axis_size("grp") - 1
    odd_one = is_odd()
    below = odd_one if odd_is_upper_group else jnp.logical_not(odd_one)
    right = jnp.where(below, jnp.maximum(group - 1, 0), jnp.minimum(group + 1, last))
    right_on = jnp.where(below, group > 0, group < last).astype(jnp.int32)

    @pl.when(below)
    def _():
        products[...] = lax.dot_general(
            y_all[:, :cut], other[...].reshape(slots * side, cut), NT, preferred_element_type=F32
        )

    @pl.when(jnp.logical_not(below))
    def _():
        products[...] = lax.dot_general(
            v_high[...], other[...].reshape(slots * side, cut), NT, preferred_element_type=F32
        )

    mine = combined(products, slots, side, ids, group, right, 1, right_on, total)
    part[...] = mine
    send[...] = mine.T.astype(BF16)


def band_kernel(middle, even, odd, got_even, got_odd, band):
    side = middle.shape[1]
    odd_one = is_odd()
    with_even = (even[...] + got_even[...].astype(F32)).astype(BF16)
    with_odd = (odd[...] + got_odd[...].astype(F32)).astype(BF16)
    band[:, :side] = jnp.where(odd_one, with_even, with_odd)
    band[:, side : 2 * side] = middle[...].astype(BF16)
    band[:, 2 * side :] = jnp.where(odd_one, with_odd, with_even)


def swapped(block, parity):
    count = lax.axis_size("grp")
    pairs = [(i, i + 1) for i in range(parity, count - 1, 2)]
    return lax.ppermute(block, "grp", pairs + [(b, a) for a, b in pairs])


def params(mib):
    return pltpu.CompilerParams(vmem_limit_bytes=mib * 1024 * 1024)


def in_hbm(x):
    return pltpu.with_memory_space_constraint(x, pltpu.HBM)


def in_vmem(x):
    return pltpu.with_memory_space_constraint(x, pltpu.VMEM)


WHOLE = pl.BlockSpec(memory_space=pltpu.VMEM)
SCALAR = pl.BlockSpec(memory_space=pltpu.SMEM)


def body(tiles, tile_ids, occ_blocks, virt_blocks):
    slots, side, flat = tiles.shape[1:]
    rows = occ_blocks.shape[0]
    members = lax.axis_size("mem")
    cut = flat // 2
    width = RIB * side

    anywhere = pl.BlockSpec(memory_space=pltpu.HBM)
    pitch = side + 8
    strided = [pltpu.VMEM((flat // (2 * side) * pitch, 2 * side), F32)] * 2
    even, odd, send_up, send_down, near, far, green = pl.pallas_call(
        send_kernel,
        in_specs=[anywhere] * 4,
        out_specs=[anywhere] * 6 + [WHOLE],
        out_shape=[
            pltpu.HBM((slots, side, cut), BF16),
            pltpu.HBM((slots, side, cut), BF16),
            jax.ShapeDtypeStruct((2, 2, flat), BF16),
            jax.ShapeDtypeStruct((1, 2, flat), BF16),
            jax.ShapeDtypeStruct((2, 2, flat), BF16),
            jax.ShapeDtypeStruct((3, 2, flat), BF16),
            jax.ShapeDtypeStruct((2, 2, side // 2, side), BF16),
        ],
        scratch_shapes=[
            pltpu.VMEM((slots, side, flat), BF16),
            pltpu.VMEM((slots, side, cut), BF16),
            pltpu.VMEM((slots, side, cut), BF16),
            pltpu.VMEM(occ_blocks.shape, BF16),
            pltpu.SMEM(tile_ids.shape, jnp.int32),
            *strided,
            pltpu.SemaphoreType.DMA((slots + 6,)),
            pltpu.SemaphoreType.DMA((slots, 2)),
        ],
        compiler_params=params(16),
    )(*(in_hbm(x) for x in (occ_blocks, tile_ids, tiles, virt_blocks)))
    got_odd = swapped(odd, 1)
    got_even = swapped(even, 0)

    macs = slots * slots * 3 * side * side * flat
    half = pl.pallas_call(
        functools.partial(half_kernel, rows),
        in_specs=[SCALAR, WHOLE, WHOLE, anywhere, anywhere],
        out_specs=WHOLE,
        out_shape=pltpu.VMEM((slots, side, flat), BF16),
        scratch_shapes=[*strided, pltpu.SemaphoreType.DMA((1,))],
        compiler_params=params(12),
        cost_estimate=pl.CostEstimate(flops=2 * macs, bytes_accessed=4 * slots * side * flat, transcendentals=0),
    )(tile_ids, green, tiles, in_hbm(even), in_hbm(odd))
    forward = [(i, i + 1) for i in range(members - 1)]
    backward = [(b, a) for a, b in forward]
    before = lax.ppermute(send_up, "mem", forward)
    after = lax.ppermute(send_down, "mem", backward)
    y_all, v_high = pl.pallas_call(
        functools.partial(prepare_kernel, rows),
        in_specs=[SCALAR] + [WHOLE] * 6,
        out_specs=[WHOLE, WHOLE],
        out_shape=[
            pltpu.VMEM((slots * 3 * side, flat), BF16),
            pltpu.VMEM((slots * 3 * side, flat - cut), BF16),
        ],
        scratch_shapes=[pltpu.VMEM((16, flat), F32), pltpu.VMEM((slots * 3, WIDE, WIDE), BF16)],
        compiler_params=params(20),
        cost_estimate=pl.CostEstimate(flops=3 * macs, bytes_accessed=10 * slots * side * flat, transcendentals=0),
    )(tile_ids, before, near, far, after, half, tiles)
    found = [
        pltpu.VMEM((RIB, side, slots * side), F32),
        pltpu.VMEM((slots * 3 * side, slots * side), F32),
    ]

    def coupled(got, odd_is_upper_group):
        return pl.pallas_call(
            functools.partial(pair_kernel, odd_is_upper_group),
            in_specs=[SCALAR] + [WHOLE] * 3,
            out_specs=[WHOLE] * 2,
            out_shape=[pltpu.VMEM((width, width), F32), pltpu.VMEM((width, width), BF16)],
            scratch_shapes=found,
            compiler_params=params(20),
            cost_estimate=pl.CostEstimate(flops=macs, bytes_accessed=8 * slots * side * flat, transcendentals=0),
        )(tile_ids, y_all, v_high, got)

    part_even, out_even = coupled(got_even, True)
    back_even = swapped(out_even, 0)
    part_odd, out_odd = coupled(got_odd, False)
    back_odd = swapped(out_odd, 1)
    middle = pl.pallas_call(
        middle_kernel,
        in_specs=[SCALAR, WHOLE, WHOLE, pl.BlockSpec(memory_space=pl.ANY)],
        out_specs=WHOLE,
        out_shape=pltpu.VMEM((width, width), F32),
        scratch_shapes=found,
        compiler_params=params(20),
        cost_estimate=pl.CostEstimate(flops=2 * macs, bytes_accessed=8 * slots * side * flat, transcendentals=0),
    )(tile_ids, y_all, tiles, out_odd)
    band = pl.pallas_call(
        band_kernel,
        in_specs=[WHOLE] * 5,
        out_specs=WHOLE,
        out_shape=jax.ShapeDtypeStruct((width, 3 * width), BF16),
        compiler_params=params(8),
    )(middle, part_even, part_odd, back_even, back_odd)
    parts = lax.all_to_all(band.reshape(members, width // members, 3 * width), "mem", 0, 0)
    return parts.astype(F32).sum(axis=0)


def solution(mesh):
    placed = (
        P("grp", "mem", None, None),
        P(None, None, "mem"),
        P("mem", None),
        P("mem", None, None),
    )
    return jax.shard_map(
        body, mesh=mesh, in_specs=placed, out_specs=P(("grp", "mem"), None), check_vma=False
    )
```

```python
import functools

import jax
import jax.numpy as jnp
from jax import lax
from jax.experimental import pallas as pl
from jax.experimental.pallas import tpu as pltpu
from jax.sharding import PartitionSpec as P

RIB = 4
WIDE = 256
F32 = jnp.float32
BF16 = jnp.bfloat16


def is_odd():
    return lax.rem(lax.axis_index("grp"), 2) == 1


def go_rows(block, source, rows_in, rows_out, result):
    side = source.shape[0]
    lanes = 2 * side
    high = source.shape[1] // lanes
    some = block.shape[0] // 2
    pitch = rows_in.shape[0] // high
    low = lax.broadcasted_iota(jnp.int32, (some, lanes), 1) < side
    for h in range(high):
        rows_in[h * pitch : h * pitch + side, :] = source[:, h * lanes : (h + 1) * lanes].astype(F32)
    for p in range(0, side, 2):
        one = rows_in[pl.ds(p, high, stride=pitch), :]
        two = rows_in[pl.ds(p + 1, high, stride=pitch), :]
        crossed = [pltpu.roll(one, side, 1), pltpu.roll(two, side, 1)]
        x = jnp.concatenate(
            [jnp.concatenate([one, two], axis=1), jnp.concatenate(crossed, axis=1)], axis=0
        )
        y = jnp.dot(block, x.astype(BF16), preferred_element_type=F32)
        rows_out[pl.ds(p, some, stride=pitch), :] = jnp.where(low, y[:some, :lanes], y[some:, :lanes])
        rows_out[pl.ds(p + 1, some, stride=pitch), :] = jnp.where(low, y[:some, lanes:], y[some:, lanes:])
    for h in range(some):
        result(slice(h * lanes, (h + 1) * lanes), rows_out[h * pitch : h * pitch + side, :].astype(BF16))


def send_kernel(
    occ_in, ids_in, tiles, virt, even, odd, send_up, send_down, near, far, green, held,
    occ, ids, rows_in, rows_out, sem
):
    slots, side, flat = held.shape
    lanes, cut = 2 * side, even.shape[2]
    high = flat // lanes
    rows = occ.shape[0]
    first_in = pltpu.make_async_copy(occ_in, occ, sem.at[slots + 2])
    ids_copy = pltpu.make_async_copy(ids_in, ids, sem.at[slots + 3])
    first_in.start()
    ids_copy.start()
    fetch = [pltpu.make_async_copy(tiles.at[0, t], held.at[t], sem.at[t]) for t in range(slots)]
    for copy in fetch:
        copy.start()
    up = pltpu.make_async_copy(virt.at[pl.ds(rows - 2, 2)], send_up, sem.at[slots])
    down = pltpu.make_async_copy(virt.at[pl.ds(0, 1)], send_down, sem.at[slots + 1])
    near_copy = pltpu.make_async_copy(virt.at[pl.ds(0, 2)], near, sem.at[slots + 4])
    far_copy = pltpu.make_async_copy(virt.at[pl.ds(rows - 3, 3)], far, sem.at[slots + 5])
    edges = [up, down, near_copy, far_copy]
    for copy in edges:
        copy.start()
    group = lax.axis_index("grp")
    first = lax.axis_index("mem") * rows
    odd_one = is_odd()
    source = lax.broadcasted_iota(jnp.int32, (lanes, side), 0)
    target = lax.broadcasted_iota(jnp.int32, (lanes, side), 1)
    mu = lax.rem(source, side)
    some = high // 2
    first_in.wait()
    for end, row in enumerate((0, rows - 1)):
        line = occ[row : row + 1, :].astype(F32)
        block = jnp.concatenate([line[:, h * lanes : (h + 1) * lanes] for h in range(high)], axis=0)
        for parity in range(2):
            other = (lax.rem(mu, 2) != parity).astype(jnp.int32)
            pick = (source // side == parity) & (target == mu // 2 + other * high)
            chosen = jnp.dot(
                block.astype(BF16), pick.astype(BF16), preferred_element_type=F32
            ).astype(BF16)
            for part in range(2):
                green[end, part, parity * some : (parity + 1) * some, :] = chosen[part * some : (part + 1) * some]
    ids_copy.wait()
    for t in range(slots):
        fetch[t].wait()
        block = green[(ids[group, 1, t] != first).astype(jnp.int32), 1]

        def result(at, done):
            raw = held[t, :, at]
            even[t, :, at] = jnp.where(odd_one, done, raw)
            odd[t, :, at] = jnp.where(odd_one, raw, done)

        go_rows(block, held.at[t], rows_in, rows_out, result)
    for copy in edges:
        copy.wait()


def half_kernel(rows, ids, green, tiles, even, odd, half, rows_in, rows_out, sem):
    slots, side, flat = half.shape
    cut = even.shape[2]
    group = lax.axis_index("grp")
    first = lax.axis_index("mem") * rows
    high_part = half.at[:, :, pl.ds(cut, flat - cut)]

    @pl.when(is_odd())
    def _():
        pltpu.make_async_copy(even, high_part, sem.at[0]).start()

    @pl.when(jnp.logical_not(is_odd()))
    def _():
        pltpu.make_async_copy(odd, high_part, sem.at[0]).start()

    for t in range(slots):
        block = green[(ids[group, 1, t] != first).astype(jnp.int32), 0]

        def result(at, done):
            half[t, :, at] = done

        go_rows(block, tiles.at[0, t], rows_in, rows_out, result)
    pltpu.make_async_copy(even, high_part, sem.at[0]).wait()


def combined(products, slots, side, ids, left, right, left_on, right_on, total):
    width = slots * side

    def spread(values, owner):
        out = jnp.full(owner.shape, values[0], jnp.int32)
        for u in range(1, slots):
            out = jnp.where(owner == u, values[u], out)
        return out

    owner = lax.broadcasted_iota(jnp.int32, (1, width), 1) // side
    live = [ids[right, 3, u] * right_on for u in range(slots)]
    row_block = spread([jnp.where(live[u] > 0, ids[right, 1, u], -1) for u in range(slots)], owner)
    col_block = spread([ids[right, 2, u] for u in range(slots)], owner)
    total[...] = jnp.zeros_like(total)
    for t in range(slots):
        same = row_block == jnp.where(ids[left, 3, t] * left_on > 0, ids[left, 1, t], -2)
        term = jnp.zeros((side, width), F32)
        for j in range(3):
            at = (t * 3 + j) * side
            match = (same & (col_block == ids[left, 2, t] + (j - 1))).astype(F32)
            term = term + products[at : at + side, :] * match
        total[ids[left, 0, t]] += term
    ahead = lax.broadcasted_iota(jnp.int32, (side, RIB * side), 1)
    ahead = ahead - lax.broadcasted_iota(jnp.int32, (side, RIB * side), 0)
    place = [(ahead == ids[right, 0, u] * side).astype(F32).astype(BF16) for u in range(slots)]
    place = jnp.concatenate(place, axis=0)
    summed = total[...].reshape(RIB * side, width)
    coarse = summed.astype(BF16)
    fine = (summed - coarse.astype(F32)).astype(BF16)
    return jnp.dot(coarse, place, preferred_element_type=F32) + jnp.dot(
        fine, place, preferred_element_type=F32
    )


NT = (((1,), (1,)), ((), ()))
NN = (((1,), (0,)), ((), ()))


def prepare_kernel(rows, ids, before, near, far, after, half, tiles, y_all, v_high, table, mats):
    slots, side, flat = half.shape
    cut = flat - v_high.shape[1]
    group = lax.axis_index("grp")
    first = lax.axis_index("mem") * rows
    count = rows * lax.axis_size("mem")
    copies = WIDE // side
    own = lax.broadcasted_iota(jnp.int32, (WIDE, WIDE), 0) // side
    own = own == lax.broadcasted_iota(jnp.int32, (WIDE, WIDE), 1) // side
    own = own.astype(F32).astype(BF16)

    at = 0
    for source in (before, near, far, after):
        for k in range(source.shape[0]):
            table[at : at + 2, :] = source[k].astype(F32)
            at += 2
    lanes = 2 * side
    pairs = side // 2
    line_of = lax.broadcasted_iota(jnp.int32, (side, pairs), 0) // 2
    line_of = (line_of == lax.broadcasted_iota(jnp.int32, (side, pairs), 1)).astype(F32).astype(BF16)
    even_row = lax.rem(lax.broadcasted_iota(jnp.int32, (side, lanes), 0), 2) == 0
    straight = even_row == (lax.broadcasted_iota(jnp.int32, (side, lanes), 1) < side)

    def spread(row, keep=None):
        line = table[pl.ds(row, 1), :]
        if keep is not None:
            line = line * keep
        block = jnp.concatenate([line[:, h * lanes : (h + 1) * lanes] for h in range(pairs)], axis=0)
        block = jnp.dot(line_of, block.astype(BF16), preferred_element_type=F32)
        block = jnp.where(straight, block, pltpu.roll(block, side, 1)).astype(BF16)
        row = jnp.concatenate([block] * (copies // 2), axis=1)
        return jnp.concatenate([row] * copies, axis=0) * own

    for t in range(slots):
        a, b = ids[group, 1, t], ids[group, 2, t]
        at = jnp.where(a == first, 2, 6) + b - a
        keep = (b + 1 < count).astype(F32)
        mats[t * 3] = spread(2 * at - 1)
        mats[t * 3 + 1] = spread(2 * at)
        mats[t * 3 + 2] = spread(2 * at + 1, keep)

    def transform(source, low, result, dims):
        lanes = result.shape[1]
        for t in range(slots):
            x = [source[t, :, c : c + WIDE] for c in range(low, low + lanes, WIDE)]
            x = jnp.concatenate(x, axis=0)
            for j in range(3):
                y = lax.dot_general(x, mats[t * 3 + j], dims[j], preferred_element_type=F32).astype(BF16)
                at = slice((t * 3 + j) * side, (t * 3 + j + 1) * side)
                for k in range(lanes // WIDE):
                    result[at, k * WIDE : (k + 1) * WIDE] = y[k * side : (k + 1) * side]

    transform(half, 0, y_all, (NT, NN, NN))
    transform(tiles.at[0], cut, v_high, (NT, NT, NN))


def middle_kernel(ids, y_all, tiles, after, middle, total, products):
    slots, side, flat = tiles.shape[1:]
    group = lax.axis_index("grp")
    products[...] = lax.dot_general(
        y_all[...], tiles[0].reshape(slots * side, flat), NT, preferred_element_type=F32
    )
    middle[...] = combined(products, slots, side, ids, group, group, 1, 1, total)


def pair_kernel(odd_is_upper_group, ids, y_all, v_high, other, part, send, total, products):
    slots, side, cut = other.shape
    group = lax.axis_index("grp")
    last = lax.axis_size("grp") - 1
    odd_one = is_odd()
    below = odd_one if odd_is_upper_group else jnp.logical_not(odd_one)
    right = jnp.where(below, jnp.maximum(group - 1, 0), jnp.minimum(group + 1, last))
    right_on = jnp.where(below, group > 0, group < last).astype(jnp.int32)

    @pl.when(below)
    def _():
        products[...] = lax.dot_general(
            y_all[:, :cut], other[...].reshape(slots * side, cut), NT, preferred_element_type=F32
        )

    @pl.when(jnp.logical_not(below))
    def _():
        products[...] = lax.dot_general(
            v_high[...], other[...].reshape(slots * side, cut), NT, preferred_element_type=F32
        )

    mine = combined(products, slots, side, ids, group, right, 1, right_on, total)
    part[...] = mine
    send[...] = mine.T.astype(BF16)


def band_kernel(middle, even, odd, got_even, got_odd, band):
    side = middle.shape[1]
    odd_one = is_odd()
    with_even = (even[...] + got_even[...].astype(F32)).astype(BF16)
    with_odd = (odd[...] + got_odd[...].astype(F32)).astype(BF16)
    band[:, :side] = jnp.where(odd_one, with_even, with_odd)
    band[:, side : 2 * side] = middle[...].astype(BF16)
    band[:, 2 * side :] = jnp.where(odd_one, with_odd, with_even)


def swapped(block, parity):
    count = lax.axis_size("grp")
    pairs = [(i, i + 1) for i in range(parity, count - 1, 2)]
    return lax.ppermute(block, "grp", pairs + [(b, a) for a, b in pairs])


def params(mib):
    return pltpu.CompilerParams(vmem_limit_bytes=mib * 1024 * 1024)


def in_hbm(x):
    return pltpu.with_memory_space_constraint(x, pltpu.HBM)


def in_vmem(x):
    return pltpu.with_memory_space_constraint(x, pltpu.VMEM)


WHOLE = pl.BlockSpec(memory_space=pltpu.VMEM)
SCALAR = pl.BlockSpec(memory_space=pltpu.SMEM)


def body(tiles, tile_ids, occ_blocks, virt_blocks):
    slots, side, flat = tiles.shape[1:]
    rows = occ_blocks.shape[0]
    members = lax.axis_size("mem")
    cut = flat // 2
    width = RIB * side

    anywhere = pl.BlockSpec(memory_space=pltpu.HBM)
    pitch = side + 8
    strided = [pltpu.VMEM((flat // (2 * side) * pitch, 2 * side), F32)] * 2
    even, odd, send_up, send_down, near, far, green = pl.pallas_call(
        send_kernel,
        in_specs=[anywhere] * 4,
        out_specs=[WHOLE] * 2 + [anywhere] * 4 + [WHOLE],
        out_shape=[
            jax.ShapeDtypeStruct((slots, side, cut), BF16),
            jax.ShapeDtypeStruct((slots, side, cut), BF16),
            jax.ShapeDtypeStruct((2, 2, flat), BF16),
            jax.ShapeDtypeStruct((1, 2, flat), BF16),
            jax.ShapeDtypeStruct((2, 2, flat), BF16),
            jax.ShapeDtypeStruct((3, 2, flat), BF16),
            jax.ShapeDtypeStruct((2, 2, side // 2, side), BF16),
        ],
        scratch_shapes=[
            pltpu.VMEM((slots, side, flat), BF16),
            pltpu.VMEM(occ_blocks.shape, BF16),
            pltpu.SMEM(tile_ids.shape, jnp.int32),
            *strided,
            pltpu.SemaphoreType.DMA((slots + 6,)),
        ],
        compiler_params=params(16),
    )(*(in_hbm(x) for x in (occ_blocks, tile_ids, tiles, virt_blocks)))
    got_odd = swapped(odd, 1)
    got_even = swapped(even, 0)

    macs = slots * slots * 3 * side * side * flat
    half = pl.pallas_call(
        functools.partial(half_kernel, rows),
        in_specs=[SCALAR, WHOLE, WHOLE] + [pl.BlockSpec(memory_space=pl.ANY)] * 2,
        out_specs=WHOLE,
        out_shape=pltpu.VMEM((slots, side, flat), BF16),
        scratch_shapes=[*strided, pltpu.SemaphoreType.DMA((1,))],
        compiler_params=params(12),
        cost_estimate=pl.CostEstimate(flops=2 * macs, bytes_accessed=4 * slots * side * flat, transcendentals=0),
    )(tile_ids, green, tiles, even, odd)
    forward = [(i, i + 1) for i in range(members - 1)]
    backward = [(b, a) for a, b in forward]
    before = lax.ppermute(send_up, "mem", forward)
    after = lax.ppermute(send_down, "mem", backward)
    y_all, v_high = pl.pallas_call(
        functools.partial(prepare_kernel, rows),
        in_specs=[SCALAR] + [WHOLE] * 6,
        out_specs=[WHOLE, WHOLE],
        out_shape=[
            pltpu.VMEM((slots * 3 * side, flat), BF16),
            pltpu.VMEM((slots * 3 * side, flat - cut), BF16),
        ],
        scratch_shapes=[pltpu.VMEM((16, flat), F32), pltpu.VMEM((slots * 3, WIDE, WIDE), BF16)],
        compiler_params=params(20),
        cost_estimate=pl.CostEstimate(flops=3 * macs, bytes_accessed=10 * slots * side * flat, transcendentals=0),
    )(tile_ids, before, near, far, after, half, tiles)
    found = [
        pltpu.VMEM((RIB, side, slots * side), F32),
        pltpu.VMEM((slots * 3 * side, slots * side), F32),
    ]

    def coupled(got, odd_is_upper_group):
        return pl.pallas_call(
            functools.partial(pair_kernel, odd_is_upper_group),
            in_specs=[SCALAR] + [WHOLE] * 3,
            out_specs=[WHOLE] * 2,
            out_shape=[pltpu.VMEM((width, width), F32), pltpu.VMEM((width, width), BF16)],
            scratch_shapes=found,
            compiler_params=params(20),
            cost_estimate=pl.CostEstimate(flops=macs, bytes_accessed=8 * slots * side * flat, transcendentals=0),
        )(tile_ids, y_all, v_high, got)

    part_even, out_even = coupled(got_even, True)
    back_even = swapped(out_even, 0)
    part_odd, out_odd = coupled(got_odd, False)
    back_odd = swapped(out_odd, 1)
    middle = pl.pallas_call(
        middle_kernel,
        in_specs=[SCALAR, WHOLE, WHOLE, pl.BlockSpec(memory_space=pl.ANY)],
        out_specs=WHOLE,
        out_shape=pltpu.VMEM((width, width), F32),
        scratch_shapes=found,
        compiler_params=params(20),
        cost_estimate=pl.CostEstimate(flops=2 * macs, bytes_accessed=8 * slots * side * flat, transcendentals=0),
    )(tile_ids, y_all, tiles, out_odd)
    band = pl.pallas_call(
        band_kernel,
        in_specs=[WHOLE] * 5,
        out_specs=WHOLE,
        out_shape=jax.ShapeDtypeStruct((width, 3 * width), BF16),
        compiler_params=params(8),
    )(middle, part_even, part_odd, back_even, back_odd)
    parts = lax.all_to_all(band.reshape(members, width // members, 3 * width), "mem", 0, 0)
    return parts.astype(F32).sum(axis=0)


def solution(mesh):
    placed = (
        P("grp", "mem", None, None),
        P(None, None, "mem"),
        P("mem", None),
        P("mem", None, None),
    )
    return jax.shard_map(
        body, mesh=mesh, in_specs=placed, out_specs=P(("grp", "mem"), None), check_vma=False
    )
```

```python
import functools

import jax
import jax.numpy as jnp
from jax import lax
from jax.experimental import pallas as pl
from jax.experimental.pallas import tpu as pltpu
from jax.sharding import PartitionSpec as P

RIB = 4
WIDE = 256
F32 = jnp.float32
BF16 = jnp.bfloat16


def is_odd():
    return lax.rem(lax.axis_index("grp"), 2) == 1


def sends_up():
    return lax.rem(lax.axis_index("grp") + lax.axis_index("mem"), 2) == 0


def go_rows(block, source, rows_in, rows_out, result):
    side = source.shape[0]
    lanes = 2 * side
    high = source.shape[1] // lanes
    some = block.shape[0] // 2
    pitch = rows_in.shape[0] // high
    low = lax.broadcasted_iota(jnp.int32, (some, lanes), 1) < side
    for h in range(high):
        rows_in[h * pitch : h * pitch + side, :] = source[:, h * lanes : (h + 1) * lanes].astype(F32)
    for p in range(0, side, 2):
        one = rows_in[pl.ds(p, high, stride=pitch), :]
        two = rows_in[pl.ds(p + 1, high, stride=pitch), :]
        crossed = [pltpu.roll(one, side, 1), pltpu.roll(two, side, 1)]
        x = jnp.concatenate(
            [jnp.concatenate([one, two], axis=1), jnp.concatenate(crossed, axis=1)], axis=0
        )
        y = jnp.dot(block, x.astype(BF16), preferred_element_type=F32)
        rows_out[pl.ds(p, some, stride=pitch), :] = jnp.where(low, y[:some, :lanes], y[some:, :lanes])
        rows_out[pl.ds(p + 1, some, stride=pitch), :] = jnp.where(low, y[:some, lanes:], y[some:, lanes:])
    for h in range(some):
        result(slice(h * lanes, (h + 1) * lanes), rows_out[h * pitch : h * pitch + side, :].astype(BF16))


def send_kernel(
    occ_in, ids_in, tiles, virt, even, odd, send_row, near, far, green, held,
    occ, ids, rows_in, rows_out, sem
):
    slots, side, flat = held.shape
    lanes, cut = 2 * side, even.shape[2]
    high = flat // lanes
    rows = occ.shape[0]
    first_in = pltpu.make_async_copy(occ_in, occ, sem.at[slots + 2])
    ids_copy = pltpu.make_async_copy(ids_in, ids, sem.at[slots + 3])
    first_in.start()
    ids_copy.start()
    fetch = [pltpu.make_async_copy(tiles.at[0, t], held.at[t], sem.at[t]) for t in range(slots)]
    for copy in fetch:
        copy.start()
    start = jnp.where(sends_up(), rows - 2, 0)
    row_copy = pltpu.make_async_copy(virt.at[pl.ds(start, 2)], send_row, sem.at[slots])
    near_copy = pltpu.make_async_copy(virt.at[pl.ds(0, 2)], near, sem.at[slots + 4])
    far_copy = pltpu.make_async_copy(virt.at[pl.ds(rows - 3, 3)], far, sem.at[slots + 5])
    edges = [row_copy, near_copy, far_copy]
    for copy in edges:
        copy.start()
    group = lax.axis_index("grp")
    first = lax.axis_index("mem") * rows
    odd_one = is_odd()
    source = lax.broadcasted_iota(jnp.int32, (lanes, side), 0)
    target = lax.broadcasted_iota(jnp.int32, (lanes, side), 1)
    mu = lax.rem(source, side)
    some = high // 2
    first_in.wait()
    for end, row in enumerate((0, rows - 1)):
        line = occ[row : row + 1, :].astype(F32)
        block = jnp.concatenate([line[:, h * lanes : (h + 1) * lanes] for h in range(high)], axis=0)
        for parity in range(2):
            other = (lax.rem(mu, 2) != parity).astype(jnp.int32)
            pick = (source // side == parity) & (target == mu // 2 + other * high)
            chosen = jnp.dot(
                block.astype(BF16), pick.astype(BF16), preferred_element_type=F32
            ).astype(BF16)
            for part in range(2):
                green[end, part, parity * some : (parity + 1) * some, :] = chosen[part * some : (part + 1) * some]
    ids_copy.wait()
    for t in range(slots):
        fetch[t].wait()
        block = green[(ids[group, 1, t] != first).astype(jnp.int32), 1]

        def result(at, done):
            raw = held[t, :, at]
            even[t, :, at] = jnp.where(odd_one, done, raw)
            odd[t, :, at] = jnp.where(odd_one, raw, done)

        go_rows(block, held.at[t], rows_in, rows_out, result)
    for copy in edges:
        copy.wait()


def half_kernel(rows, ids, green, tiles, even, odd, half, rows_in, rows_out, sem):
    slots, side, flat = half.shape
    cut = even.shape[2]
    group = lax.axis_index("grp")
    first = lax.axis_index("mem") * rows
    high_part = half.at[:, :, pl.ds(cut, flat - cut)]

    @pl.when(is_odd())
    def _():
        pltpu.make_async_copy(even, high_part, sem.at[0]).start()

    @pl.when(jnp.logical_not(is_odd()))
    def _():
        pltpu.make_async_copy(odd, high_part, sem.at[0]).start()

    for t in range(slots):
        block = green[(ids[group, 1, t] != first).astype(jnp.int32), 0]

        def result(at, done):
            half[t, :, at] = done

        go_rows(block, tiles.at[0, t], rows_in, rows_out, result)
    pltpu.make_async_copy(even, high_part, sem.at[0]).wait()


def combined(products, slots, side, ids, left, right, left_on, right_on, total):
    width = slots * side

    def spread(values, owner):
        out = jnp.full(owner.shape, values[0], jnp.int32)
        for u in range(1, slots):
            out = jnp.where(owner == u, values[u], out)
        return out

    owner = lax.broadcasted_iota(jnp.int32, (1, width), 1) // side
    live = [ids[right, 3, u] * right_on for u in range(slots)]
    row_block = spread([jnp.where(live[u] > 0, ids[right, 1, u], -1) for u in range(slots)], owner)
    col_block = spread([ids[right, 2, u] for u in range(slots)], owner)
    total[...] = jnp.zeros_like(total)
    for t in range(slots):
        same = row_block == jnp.where(ids[left, 3, t] * left_on > 0, ids[left, 1, t], -2)
        term = jnp.zeros((side, width), F32)
        for j in range(3):
            at = (t * 3 + j) * side
            match = (same & (col_block == ids[left, 2, t] + (j - 1))).astype(F32)
            term = term + products[at : at + side, :] * match
        total[ids[left, 0, t]] += term
    ahead = lax.broadcasted_iota(jnp.int32, (side, RIB * side), 1)
    ahead = ahead - lax.broadcasted_iota(jnp.int32, (side, RIB * side), 0)
    place = [(ahead == ids[right, 0, u] * side).astype(F32).astype(BF16) for u in range(slots)]
    place = jnp.concatenate(place, axis=0)
    summed = total[...].reshape(RIB * side, width)
    coarse = summed.astype(BF16)
    fine = (summed - coarse.astype(F32)).astype(BF16)
    return jnp.dot(coarse, place, preferred_element_type=F32) + jnp.dot(
        fine, place, preferred_element_type=F32
    )


NT = (((1,), (1,)), ((), ()))
NN = (((1,), (0,)), ((), ()))


def prepare_kernel(rows, ids, fetched, passed, near, far, half, tiles, y_all, v_high, table, mats):
    slots, side, flat = half.shape
    cut = flat - v_high.shape[1]
    group = lax.axis_index("grp")
    first = lax.axis_index("mem") * rows
    count = rows * lax.axis_size("mem")
    copies = WIDE // side
    own = lax.broadcasted_iota(jnp.int32, (WIDE, WIDE), 0) // side
    own = own == lax.broadcasted_iota(jnp.int32, (WIDE, WIDE), 1) // side
    own = own.astype(F32).astype(BF16)

    from_above = sends_up()
    for k in range(2):
        one, two = fetched[k].astype(F32), passed[k].astype(F32)
        table[2 * k : 2 * k + 2, :] = jnp.where(from_above, two, one)
        table[2 * k + 4 : 2 * k + 6, :] = near[k].astype(F32)
        if k == 0:
            table[14:16, :] = jnp.where(from_above, one, two)
    for k in range(3):
        table[2 * k + 8 : 2 * k + 10, :] = far[k].astype(F32)
    lanes = 2 * side
    pairs = side // 2
    line_of = lax.broadcasted_iota(jnp.int32, (side, pairs), 0) // 2
    line_of = (line_of == lax.broadcasted_iota(jnp.int32, (side, pairs), 1)).astype(F32).astype(BF16)
    even_row = lax.rem(lax.broadcasted_iota(jnp.int32, (side, lanes), 0), 2) == 0
    straight = even_row == (lax.broadcasted_iota(jnp.int32, (side, lanes), 1) < side)

    def spread(row, keep=None):
        line = table[pl.ds(row, 1), :]
        if keep is not None:
            line = line * keep
        block = jnp.concatenate([line[:, h * lanes : (h + 1) * lanes] for h in range(pairs)], axis=0)
        block = jnp.dot(line_of, block.astype(BF16), preferred_element_type=F32)
        block = jnp.where(straight, block, pltpu.roll(block, side, 1)).astype(BF16)
        row = jnp.concatenate([block] * (copies // 2), axis=1)
        return jnp.concatenate([row] * copies, axis=0) * own

    for t in range(slots):
        a, b = ids[group, 1, t], ids[group, 2, t]
        at = jnp.where(a == first, 2, 6) + b - a
        keep = (b + 1 < count).astype(F32)
        mats[t * 3] = spread(2 * at - 1)
        mats[t * 3 + 1] = spread(2 * at)
        mats[t * 3 + 2] = spread(2 * at + 1, keep)

    def transform(source, low, result, dims):
        lanes = result.shape[1]
        for t in range(slots):
            x = [source[t, :, c : c + WIDE] for c in range(low, low + lanes, WIDE)]
            x = jnp.concatenate(x, axis=0)
            for j in range(3):
                y = lax.dot_general(x, mats[t * 3 + j], dims[j], preferred_element_type=F32).astype(BF16)
                at = slice((t * 3 + j) * side, (t * 3 + j + 1) * side)
                for k in range(lanes // WIDE):
                    result[at, k * WIDE : (k + 1) * WIDE] = y[k * side : (k + 1) * side]

    transform(half, 0, y_all, (NT, NN, NN))
    transform(tiles.at[0], cut, v_high, (NT, NT, NN))


def middle_kernel(ids, y_all, tiles, after, middle, total, products):
    slots, side, flat = tiles.shape[1:]
    group = lax.axis_index("grp")
    products[...] = lax.dot_general(
        y_all[...], tiles[0].reshape(slots * side, flat), NT, preferred_element_type=F32
    )
    middle[...] = combined(products, slots, side, ids, group, group, 1, 1, total)


def pair_kernel(odd_is_upper_group, ids, y_all, v_high, other, part, send, total, products):
    slots, side, cut = other.shape
    group = lax.axis_index("grp")
    last = lax.axis_size("grp") - 1
    odd_one = is_odd()
    below = odd_one if odd_is_upper_group else jnp.logical_not(odd_one)
    right = jnp.where(below, jnp.maximum(group - 1, 0), jnp.minimum(group + 1, last))
    right_on = jnp.where(below, group > 0, group < last).astype(jnp.int32)

    @pl.when(below)
    def _():
        products[...] = lax.dot_general(
            y_all[:, :cut], other[...].reshape(slots * side, cut), NT, preferred_element_type=F32
        )

    @pl.when(jnp.logical_not(below))
    def _():
        products[...] = lax.dot_general(
            v_high[...], other[...].reshape(slots * side, cut), NT, preferred_element_type=F32
        )

    mine = combined(products, slots, side, ids, group, right, 1, right_on, total)
    part[...] = mine
    send[...] = mine.T.astype(BF16)


def band_kernel(middle, even, odd, got_even, got_odd, band):
    side = middle.shape[1]
    odd_one = is_odd()
    with_even = (even[...] + got_even[...].astype(F32)).astype(BF16)
    with_odd = (odd[...] + got_odd[...].astype(F32)).astype(BF16)
    band[:, :side] = jnp.where(odd_one, with_even, with_odd)
    band[:, side : 2 * side] = middle[...].astype(BF16)
    band[:, 2 * side :] = jnp.where(odd_one, with_odd, with_even)


def swapped(block, parity):
    count = lax.axis_size("grp")
    pairs = [(i, i + 1) for i in range(parity, count - 1, 2)]
    return lax.ppermute(block, "grp", pairs + [(b, a) for a, b in pairs])


def params(mib):
    return pltpu.CompilerParams(vmem_limit_bytes=mib * 1024 * 1024)


def in_hbm(x):
    return pltpu.with_memory_space_constraint(x, pltpu.HBM)


def in_vmem(x):
    return pltpu.with_memory_space_constraint(x, pltpu.VMEM)


WHOLE = pl.BlockSpec(memory_space=pltpu.VMEM)
SCALAR = pl.BlockSpec(memory_space=pltpu.SMEM)


def body(tiles, tile_ids, occ_blocks, virt_blocks):
    slots, side, flat = tiles.shape[1:]
    rows = occ_blocks.shape[0]
    members = lax.axis_size("mem")
    cut = flat // 2
    width = RIB * side

    anywhere = pl.BlockSpec(memory_space=pltpu.HBM)
    pitch = side + 8
    strided = [pltpu.VMEM((flat // (2 * side) * pitch, 2 * side), F32)] * 2
    even, odd, send_row, near, far, green = pl.pallas_call(
        send_kernel,
        in_specs=[anywhere] * 4,
        out_specs=[WHOLE] * 2 + [anywhere] * 3 + [WHOLE],
        out_shape=[
            jax.ShapeDtypeStruct((slots, side, cut), BF16),
            jax.ShapeDtypeStruct((slots, side, cut), BF16),
            jax.ShapeDtypeStruct((2, 2, flat), BF16),
            jax.ShapeDtypeStruct((2, 2, flat), BF16),
            jax.ShapeDtypeStruct((3, 2, flat), BF16),
            jax.ShapeDtypeStruct((2, 2, side // 2, side), BF16),
        ],
        scratch_shapes=[
            pltpu.VMEM((slots, side, flat), BF16),
            pltpu.VMEM(occ_blocks.shape, BF16),
            pltpu.SMEM(tile_ids.shape, jnp.int32),
            *strided,
            pltpu.SemaphoreType.DMA((slots + 6,)),
        ],
        compiler_params=params(16),
    )(*(in_hbm(x) for x in (occ_blocks, tile_ids, tiles, virt_blocks)))
    got_odd = swapped(odd, 1)
    got_even = swapped(even, 0)

    macs = slots * slots * 3 * side * side * flat
    half = pl.pallas_call(
        functools.partial(half_kernel, rows),
        in_specs=[SCALAR, WHOLE, WHOLE] + [pl.BlockSpec(memory_space=pl.ANY)] * 2,
        out_specs=WHOLE,
        out_shape=pltpu.VMEM((slots, side, flat), BF16),
        scratch_shapes=[*strided, pltpu.SemaphoreType.DMA((1,))],
        compiler_params=params(12),
        cost_estimate=pl.CostEstimate(flops=2 * macs, bytes_accessed=4 * slots * side * flat, transcendentals=0),
    )(tile_ids, green, tiles, even, odd)
    route = []
    for g in range(lax.axis_size("grp")):
        for m in range(g % 2, members - 1, 2):
            a, b = g * members + m, g * members + m + 1
            route += [(a, b), (b, a)]
    fetched = lax.ppermute(send_row, ("grp", "mem"), route)
    macs = slots * slots * 3 * side * side * flat
    half = pl.pallas_call(
        functools.partial(half_kernel, rows),
        in_specs=[SCALAR, WHOLE, WHOLE] + [pl.BlockSpec(memory_space=pl.ANY)] * 2,
        out_specs=WHOLE,
        out_shape=pltpu.VMEM((slots, side, flat), BF16),
        scratch_shapes=[*strided, pltpu.SemaphoreType.DMA((1,))],
        compiler_params=params(12),
        cost_estimate=pl.CostEstimate(flops=2 * macs, bytes_accessed=4 * slots * side * flat, transcendentals=0),
    )(tile_ids, green, tiles, even, odd)
    forward = [(i, i + 1) for i in range(members - 1)]
    backward = [(b, a) for a, b in forward]
    fetched, half = lax.optimization_barrier((fetched, half))
    passed = swapped(fetched, 0)
    y_all, v_high = pl.pallas_call(
        functools.partial(prepare_kernel, rows),
        in_specs=[SCALAR] + [WHOLE] * 6,
        out_specs=[WHOLE, WHOLE],
        out_shape=[
            pltpu.VMEM((slots * 3 * side, flat), BF16),
            pltpu.VMEM((slots * 3 * side, flat - cut), BF16),
        ],
        scratch_shapes=[pltpu.VMEM((16, flat), F32), pltpu.VMEM((slots * 3, WIDE, WIDE), BF16)],
        compiler_params=params(20),
        cost_estimate=pl.CostEstimate(flops=3 * macs, bytes_accessed=10 * slots * side * flat, transcendentals=0),
    )(tile_ids, fetched, passed, near, far, half, tiles)
    found = [
        pltpu.VMEM((RIB, side, slots * side), F32),
        pltpu.VMEM((slots * 3 * side, slots * side), F32),
    ]

    def coupled(got, odd_is_upper_group):
        return pl.pallas_call(
            functools.partial(pair_kernel, odd_is_upper_group),
            in_specs=[SCALAR] + [WHOLE] * 3,
            out_specs=[WHOLE] * 2,
            out_shape=[pltpu.VMEM((width, width), F32), pltpu.VMEM((width, width), BF16)],
            scratch_shapes=found,
            compiler_params=params(20),
            cost_estimate=pl.CostEstimate(flops=macs, bytes_accessed=8 * slots * side * flat, transcendentals=0),
        )(tile_ids, y_all, v_high, got)

    part_even, out_even = coupled(got_even, True)
    back_even = swapped(out_even, 0)
    part_odd, out_odd = coupled(got_odd, False)
    back_odd = swapped(out_odd, 1)
    middle = pl.pallas_call(
        middle_kernel,
        in_specs=[SCALAR, WHOLE, WHOLE, pl.BlockSpec(memory_space=pl.ANY)],
        out_specs=WHOLE,
        out_shape=pltpu.VMEM((width, width), F32),
        scratch_shapes=found,
        compiler_params=params(20),
        cost_estimate=pl.CostEstimate(flops=2 * macs, bytes_accessed=8 * slots * side * flat, transcendentals=0),
    )(tile_ids, y_all, tiles, out_odd)
    band = pl.pallas_call(
        band_kernel,
        in_specs=[WHOLE] * 5,
        out_specs=WHOLE,
        out_shape=jax.ShapeDtypeStruct((width, 3 * width), BF16),
        compiler_params=params(8),
    )(middle, part_even, part_odd, back_even, back_odd)
    parts = lax.all_to_all(band.reshape(members, width // members, 3 * width), "mem", 0, 0)
    return parts.astype(F32).sum(axis=0)


def solution(mesh):
    placed = (
        P("grp", "mem", None, None),
        P(None, None, "mem"),
        P("mem", None),
        P("mem", None, None),
    )
    return jax.shard_map(
        body, mesh=mesh, in_specs=placed, out_specs=P(("grp", "mem"), None), check_vma=False
    )
```

```python
import functools

import jax
import jax.numpy as jnp
from jax import lax
from jax.experimental import pallas as pl
from jax.experimental.pallas import tpu as pltpu
from jax.sharding import PartitionSpec as P

RIB = 4
WIDE = 256
F32 = jnp.float32
BF16 = jnp.bfloat16


def is_odd():
    return lax.rem(lax.axis_index("grp"), 2) == 1


def sends_up():
    return lax.rem(lax.axis_index("grp") + lax.axis_index("mem"), 2) == 0


def go_rows(block, source, rows_in, rows_out, result):
    side = source.shape[0]
    lanes = 2 * side
    high = source.shape[1] // lanes
    some = block.shape[0] // 2
    pitch = rows_in.shape[0] // high
    low = lax.broadcasted_iota(jnp.int32, (some, lanes), 1) < side
    for h in range(high):
        rows_in[h * pitch : h * pitch + side, :] = source[:, h * lanes : (h + 1) * lanes].astype(F32)
    for p in range(0, side, 2):
        one = rows_in[pl.ds(p, high, stride=pitch), :]
        two = rows_in[pl.ds(p + 1, high, stride=pitch), :]
        crossed = [pltpu.roll(one, side, 1), pltpu.roll(two, side, 1)]
        x = jnp.concatenate(
            [jnp.concatenate([one, two], axis=1), jnp.concatenate(crossed, axis=1)], axis=0
        )
        y = jnp.dot(block, x.astype(BF16), preferred_element_type=F32)
        rows_out[pl.ds(p, some, stride=pitch), :] = jnp.where(low, y[:some, :lanes], y[some:, :lanes])
        rows_out[pl.ds(p + 1, some, stride=pitch), :] = jnp.where(low, y[:some, lanes:], y[some:, lanes:])
    for h in range(some):
        result(slice(h * lanes, (h + 1) * lanes), rows_out[h * pitch : h * pitch + side, :].astype(BF16))


def send_kernel(
    occ_in, ids_in, tiles, virt, even, odd, send_row, near, far, green, held,
    occ, ids, rows_in, rows_out, sem
):
    slots, side, flat = held.shape
    lanes, cut = 2 * side, even.shape[2]
    high = flat // lanes
    rows = occ.shape[0]
    first_in = pltpu.make_async_copy(occ_in, occ, sem.at[slots + 2])
    ids_copy = pltpu.make_async_copy(ids_in, ids, sem.at[slots + 3])
    first_in.start()
    ids_copy.start()
    fetch = [pltpu.make_async_copy(tiles.at[0, t], held.at[t], sem.at[t]) for t in range(slots)]
    for copy in fetch:
        copy.start()
    start = jnp.where(sends_up(), rows - 2, 0)
    row_copy = pltpu.make_async_copy(virt.at[pl.ds(start, 2)], send_row, sem.at[slots])
    near_copy = pltpu.make_async_copy(virt.at[pl.ds(0, 2)], near, sem.at[slots + 4])
    far_copy = pltpu.make_async_copy(virt.at[pl.ds(rows - 3, 3)], far, sem.at[slots + 5])
    edges = [row_copy, near_copy, far_copy]
    for copy in edges:
        copy.start()
    group = lax.axis_index("grp")
    first = lax.axis_index("mem") * rows
    odd_one = is_odd()
    source = lax.broadcasted_iota(jnp.int32, (lanes, side), 0)
    target = lax.broadcasted_iota(jnp.int32, (lanes, side), 1)
    mu = lax.rem(source, side)
    some = high // 2
    first_in.wait()
    for end, row in enumerate((0, rows - 1)):
        line = occ[row : row + 1, :].astype(F32)
        block = jnp.concatenate([line[:, h * lanes : (h + 1) * lanes] for h in range(high)], axis=0)
        for parity in range(2):
            other = (lax.rem(mu, 2) != parity).astype(jnp.int32)
            pick = (source // side == parity) & (target == mu // 2 + other * high)
            chosen = jnp.dot(
                block.astype(BF16), pick.astype(BF16), preferred_element_type=F32
            ).astype(BF16)
            for part in range(2):
                green[end, part, parity * some : (parity + 1) * some, :] = chosen[part * some : (part + 1) * some]
    ids_copy.wait()
    for t in range(slots):
        fetch[t].wait()
        block = green[(ids[group, 1, t] != first).astype(jnp.int32), 1]

        def result(at, done):
            raw = held[t, :, at]
            even[t, :, at] = jnp.where(odd_one, done, raw)
            odd[t, :, at] = jnp.where(odd_one, raw, done)

        go_rows(block, held.at[t], rows_in, rows_out, result)
    for copy in edges:
        copy.wait()


def half_kernel(rows, ids, green, tiles, even, odd, half, rows_in, rows_out, sem):
    slots, side, flat = half.shape
    cut = even.shape[2]
    group = lax.axis_index("grp")
    first = lax.axis_index("mem") * rows
    high_part = half.at[:, :, pl.ds(cut, flat - cut)]

    @pl.when(is_odd())
    def _():
        pltpu.make_async_copy(even, high_part, sem.at[0]).start()

    @pl.when(jnp.logical_not(is_odd()))
    def _():
        pltpu.make_async_copy(odd, high_part, sem.at[0]).start()

    for t in range(slots):
        block = green[(ids[group, 1, t] != first).astype(jnp.int32), 0]

        def result(at, done):
            half[t, :, at] = done

        go_rows(block, tiles.at[0, t], rows_in, rows_out, result)
    pltpu.make_async_copy(even, high_part, sem.at[0]).wait()


def combined(products, slots, side, ids, left, right, total):
    width = slots * side

    def spread(values, owner):
        out = jnp.full(owner.shape, values[0], jnp.int32)
        for u in range(1, slots):
            out = jnp.where(owner == u, values[u], out)
        return out

    owner = lax.broadcasted_iota(jnp.int32, (1, width), 1) // side
    live = [jnp.where(ids[right, 3, u] > 0, ids[right, 1, u], -1) for u in range(slots)]
    row_block = spread(live, owner)
    col_block = spread([ids[right, 2, u] for u in range(slots)], owner)
    total[...] = jnp.zeros_like(total)
    for t in range(slots):
        same = row_block == jnp.where(ids[left, 3, t] > 0, ids[left, 1, t], -2)
        term = jnp.zeros((side, width), F32)
        for j in range(3):
            at = (t * 3 + j) * side
            match = (same & (col_block == ids[left, 2, t] + (j - 1))).astype(F32)
            term = term + products[at : at + side, :] * match
        total[ids[left, 0, t]] += term
    ahead = lax.broadcasted_iota(jnp.int32, (side, RIB * side), 1)
    ahead = ahead - lax.broadcasted_iota(jnp.int32, (side, RIB * side), 0)
    place = [(ahead == ids[right, 0, u] * side).astype(F32).astype(BF16) for u in range(slots)]
    place = jnp.concatenate(place, axis=0)
    summed = total[...].reshape(RIB * side, width)
    coarse = summed.astype(BF16)
    fine = (summed - coarse.astype(F32)).astype(BF16)
    return jnp.dot(coarse, place, preferred_element_type=F32) + jnp.dot(
        fine, place, preferred_element_type=F32
    )


NT = (((1,), (1,)), ((), ()))
NN = (((1,), (0,)), ((), ()))


def prepare_kernel(rows, ids, fetched, passed, near, far, half, tiles, y_all, v_high, table, mats):
    slots, side, flat = half.shape
    cut = flat - v_high.shape[1]
    group = lax.axis_index("grp")
    first = lax.axis_index("mem") * rows
    count = rows * lax.axis_size("mem")
    copies = WIDE // side
    own = lax.broadcasted_iota(jnp.int32, (WIDE, WIDE), 0) // side
    own = own == lax.broadcasted_iota(jnp.int32, (WIDE, WIDE), 1) // side
    own = own.astype(F32).astype(BF16)

    from_above = sends_up()
    for k in range(2):
        one, two = fetched[k].astype(F32), passed[k].astype(F32)
        table[2 * k : 2 * k + 2, :] = jnp.where(from_above, two, one)
        table[2 * k + 4 : 2 * k + 6, :] = near[k].astype(F32)
        if k == 0:
            table[14:16, :] = jnp.where(from_above, one, two)
    for k in range(3):
        table[2 * k + 8 : 2 * k + 10, :] = far[k].astype(F32)
    lanes = 2 * side
    pairs = side // 2
    line_of = lax.broadcasted_iota(jnp.int32, (side, pairs), 0) // 2
    line_of = (line_of == lax.broadcasted_iota(jnp.int32, (side, pairs), 1)).astype(F32).astype(BF16)
    even_row = lax.rem(lax.broadcasted_iota(jnp.int32, (side, lanes), 0), 2) == 0
    straight = even_row == (lax.broadcasted_iota(jnp.int32, (side, lanes), 1) < side)

    def spread(row, keep=None):
        line = table[pl.ds(row, 1), :]
        if keep is not None:
            line = line * keep
        block = jnp.concatenate([line[:, h * lanes : (h + 1) * lanes] for h in range(pairs)], axis=0)
        block = jnp.dot(line_of, block.astype(BF16), preferred_element_type=F32)
        block = jnp.where(straight, block, pltpu.roll(block, side, 1)).astype(BF16)
        row = jnp.concatenate([block] * (copies // 2), axis=1)
        return jnp.concatenate([row] * copies, axis=0) * own

    for t in range(slots):
        a, b = ids[group, 1, t], ids[group, 2, t]
        at = jnp.where(a == first, 2, 6) + b - a
        keep = (b + 1 < count).astype(F32)
        mats[t * 3] = spread(2 * at - 1)
        mats[t * 3 + 1] = spread(2 * at)
        mats[t * 3 + 2] = spread(2 * at + 1, keep)

    def transform(source, low, result, dims):
        lanes = result.shape[1]
        for t in range(slots):
            x = [source[t, :, c : c + WIDE] for c in range(low, low + lanes, WIDE)]
            x = jnp.concatenate(x, axis=0)
            for j in range(3):
                y = lax.dot_general(x, mats[t * 3 + j], dims[j], preferred_element_type=F32).astype(BF16)
                at = slice((t * 3 + j) * side, (t * 3 + j + 1) * side)
                for k in range(lanes // WIDE):
                    result[at, k * WIDE : (k + 1) * WIDE] = y[k * side : (k + 1) * side]

    transform(half, 0, y_all, (NT, NN, NN))
    transform(tiles.at[0], cut, v_high, (NT, NT, NN))


def middle_kernel(ids, y_all, tiles, after, middle, total, products):
    slots, side, flat = tiles.shape[1:]
    group = lax.axis_index("grp")
    products[...] = lax.dot_general(
        y_all[...], tiles[0].reshape(slots * side, flat), NT, preferred_element_type=F32
    )
    middle[...] = combined(products, slots, side, ids, group, group, total)


def pair_kernel(odd_is_upper_group, ids, y_all, v_high, other, part, send, total, products):
    slots, side, cut = other.shape
    group = lax.axis_index("grp")
    last = lax.axis_size("grp") - 1
    odd_one = is_odd()
    below = odd_one if odd_is_upper_group else jnp.logical_not(odd_one)
    right = jnp.where(below, jnp.maximum(group - 1, 0), jnp.minimum(group + 1, last))
    exists = jnp.where(below, group, last - group) > 0
    partner = other[...].reshape(slots * side, cut)

    @pl.when(exists & below)
    def _():
        products[...] = lax.dot_general(y_all[:, :cut], partner, NT, preferred_element_type=F32)

    @pl.when(exists & jnp.logical_not(below))
    def _():
        products[...] = lax.dot_general(v_high[...], partner, NT, preferred_element_type=F32)

    @pl.when(exists)
    def _():
        mine = combined(products, slots, side, ids, group, right, total)
        part[...] = mine
        send[...] = mine.T.astype(BF16)

    @pl.when(jnp.logical_not(exists))
    def _():
        part[...] = jnp.zeros_like(part)
        send[...] = jnp.zeros_like(send)


def band_kernel(middle, even, odd, got_even, got_odd, band):
    side = middle.shape[1]
    odd_one = is_odd()
    with_even = (even[...] + got_even[...].astype(F32)).astype(BF16)
    with_odd = (odd[...] + got_odd[...].astype(F32)).astype(BF16)
    band[:, :side] = jnp.where(odd_one, with_even, with_odd)
    band[:, side : 2 * side] = middle[...].astype(BF16)
    band[:, 2 * side :] = jnp.where(odd_one, with_odd, with_even)


def swapped(block, parity):
    count = lax.axis_size("grp")
    pairs = [(i, i + 1) for i in range(parity, count - 1, 2)]
    return lax.ppermute(block, "grp", pairs + [(b, a) for a, b in pairs])


def params(mib):
    return pltpu.CompilerParams(vmem_limit_bytes=mib * 1024 * 1024)


def in_hbm(x):
    return pltpu.with_memory_space_constraint(x, pltpu.HBM)


def in_vmem(x):
    return pltpu.with_memory_space_constraint(x, pltpu.VMEM)


WHOLE = pl.BlockSpec(memory_space=pltpu.VMEM)
SCALAR = pl.BlockSpec(memory_space=pltpu.SMEM)


def body(tiles, tile_ids, occ_blocks, virt_blocks):
    slots, side, flat = tiles.shape[1:]
    rows = occ_blocks.shape[0]
    members = lax.axis_size("mem")
    cut = flat // 2
    width = RIB * side

    anywhere = pl.BlockSpec(memory_space=pltpu.HBM)
    pitch = side + 8
    strided = [pltpu.VMEM((flat // (2 * side) * pitch, 2 * side), F32)] * 2
    even, odd, send_row, near, far, green = pl.pallas_call(
        send_kernel,
        in_specs=[anywhere] * 4,
        out_specs=[WHOLE] * 2 + [anywhere] * 3 + [WHOLE],
        out_shape=[
            jax.ShapeDtypeStruct((slots, side, cut), BF16),
            jax.ShapeDtypeStruct((slots, side, cut), BF16),
            jax.ShapeDtypeStruct((2, 2, flat), BF16),
            jax.ShapeDtypeStruct((2, 2, flat), BF16),
            jax.ShapeDtypeStruct((3, 2, flat), BF16),
            jax.ShapeDtypeStruct((2, 2, side // 2, side), BF16),
        ],
        scratch_shapes=[
            pltpu.VMEM((slots, side, flat), BF16),
            pltpu.VMEM(occ_blocks.shape, BF16),
            pltpu.SMEM(tile_ids.shape, jnp.int32),
            *strided,
            pltpu.SemaphoreType.DMA((slots + 6,)),
        ],
        compiler_params=params(16),
    )(*(in_hbm(x) for x in (occ_blocks, tile_ids, tiles, virt_blocks)))
    got_odd = swapped(odd, 1)
    got_even = swapped(even, 0)

    macs = slots * slots * 3 * side * side * flat
    half = pl.pallas_call(
        functools.partial(half_kernel, rows),
        in_specs=[SCALAR, WHOLE, WHOLE] + [pl.BlockSpec(memory_space=pl.ANY)] * 2,
        out_specs=WHOLE,
        out_shape=pltpu.VMEM((slots, side, flat), BF16),
        scratch_shapes=[*strided, pltpu.SemaphoreType.DMA((1,))],
        compiler_params=params(12),
        cost_estimate=pl.CostEstimate(flops=2 * macs, bytes_accessed=4 * slots * side * flat, transcendentals=0),
    )(tile_ids, green, tiles, even, odd)
    route = []
    for g in range(lax.axis_size("grp")):
        for m in range(g % 2, members - 1, 2):
            a, b = g * members + m, g * members + m + 1
            route += [(a, b), (b, a)]
    fetched = lax.ppermute(send_row, ("grp", "mem"), route)
    macs = slots * slots * 3 * side * side * flat
    half = pl.pallas_call(
        functools.partial(half_kernel, rows),
        in_specs=[SCALAR, WHOLE, WHOLE] + [pl.BlockSpec(memory_space=pl.ANY)] * 2,
        out_specs=WHOLE,
        out_shape=pltpu.VMEM((slots, side, flat), BF16),
        scratch_shapes=[*strided, pltpu.SemaphoreType.DMA((1,))],
        compiler_params=params(12),
        cost_estimate=pl.CostEstimate(flops=2 * macs, bytes_accessed=4 * slots * side * flat, transcendentals=0),
    )(tile_ids, green, tiles, even, odd)
    forward = [(i, i + 1) for i in range(members - 1)]
    backward = [(b, a) for a, b in forward]
    fetched, half = lax.optimization_barrier((fetched, half))
    passed = swapped(fetched, 0)
    y_all, v_high = pl.pallas_call(
        functools.partial(prepare_kernel, rows),
        in_specs=[SCALAR] + [WHOLE] * 6,
        out_specs=[WHOLE, WHOLE],
        out_shape=[
            pltpu.VMEM((slots * 3 * side, flat), BF16),
            pltpu.VMEM((slots * 3 * side, flat - cut), BF16),
        ],
        scratch_shapes=[pltpu.VMEM((16, flat), F32), pltpu.VMEM((slots * 3, WIDE, WIDE), BF16)],
        compiler_params=params(20),
        cost_estimate=pl.CostEstimate(flops=3 * macs, bytes_accessed=10 * slots * side * flat, transcendentals=0),
    )(tile_ids, fetched, passed, near, far, half, tiles)
    found = [
        pltpu.VMEM((RIB, side, slots * side), F32),
        pltpu.VMEM((slots * 3 * side, slots * side), F32),
    ]

    def coupled(got, odd_is_upper_group):
        return pl.pallas_call(
            functools.partial(pair_kernel, odd_is_upper_group),
            in_specs=[SCALAR] + [WHOLE] * 3,
            out_specs=[WHOLE] * 2,
            out_shape=[pltpu.VMEM((width, width), F32), pltpu.VMEM((width, width), BF16)],
            scratch_shapes=found,
            compiler_params=params(20),
            cost_estimate=pl.CostEstimate(flops=macs, bytes_accessed=8 * slots * side * flat, transcendentals=0),
        )(tile_ids, y_all, v_high, got)

    part_even, out_even = coupled(got_even, True)
    back_even = swapped(out_even, 0)
    part_odd, out_odd = coupled(got_odd, False)
    back_odd = swapped(out_odd, 1)
    middle = pl.pallas_call(
        middle_kernel,
        in_specs=[SCALAR, WHOLE, WHOLE, pl.BlockSpec(memory_space=pl.ANY)],
        out_specs=WHOLE,
        out_shape=pltpu.VMEM((width, width), F32),
        scratch_shapes=found,
        compiler_params=params(20),
        cost_estimate=pl.CostEstimate(flops=2 * macs, bytes_accessed=8 * slots * side * flat, transcendentals=0),
    )(tile_ids, y_all, tiles, out_odd)
    band = pl.pallas_call(
        band_kernel,
        in_specs=[WHOLE] * 5,
        out_specs=WHOLE,
        out_shape=jax.ShapeDtypeStruct((width, 3 * width), BF16),
        compiler_params=params(8),
    )(middle, part_even, part_odd, back_even, back_odd)
    parts = lax.all_to_all(band.reshape(members, width // members, 3 * width), "mem", 0, 0)
    return parts.astype(F32).sum(axis=0)


def solution(mesh):
    placed = (
        P("grp", "mem", None, None),
        P(None, None, "mem"),
        P("mem", None),
        P("mem", None, None),
    )
    return jax.shard_map(
        body, mesh=mesh, in_specs=placed, out_specs=P(("grp", "mem"), None), check_vma=False
    )
```

```python
import functools

import jax
import jax.numpy as jnp
from jax import lax
from jax.experimental import pallas as pl
from jax.experimental.pallas import tpu as pltpu
from jax.sharding import PartitionSpec as P

RIB = 4
WIDE = 256
F32 = jnp.float32
BF16 = jnp.bfloat16


def is_odd():
    return lax.rem(lax.axis_index("grp"), 2) == 1


def sends_up():
    return lax.rem(lax.axis_index("grp") + lax.axis_index("mem"), 2) == 0


def go_rows(block, source, rows_in, rows_out, result):
    side = source.shape[0]
    lanes = 2 * side
    high = source.shape[1] // lanes
    some = block.shape[0] // 2
    pitch = rows_in.shape[0] // high
    low = lax.broadcasted_iota(jnp.int32, (some, lanes), 1) < side
    for h in range(high):
        rows_in[h * pitch : h * pitch + side, :] = source[:, h * lanes : (h + 1) * lanes].astype(F32)
    for p in range(0, side, 2):
        one = rows_in[pl.ds(p, high, stride=pitch), :]
        two = rows_in[pl.ds(p + 1, high, stride=pitch), :]
        crossed = [pltpu.roll(one, side, 1), pltpu.roll(two, side, 1)]
        x = jnp.concatenate(
            [jnp.concatenate([one, two], axis=1), jnp.concatenate(crossed, axis=1)], axis=0
        )
        y = jnp.dot(block, x.astype(BF16), preferred_element_type=F32)
        rows_out[pl.ds(p, some, stride=pitch), :] = jnp.where(low, y[:some, :lanes], y[some:, :lanes])
        rows_out[pl.ds(p + 1, some, stride=pitch), :] = jnp.where(low, y[:some, lanes:], y[some:, lanes:])
    for h in range(some):
        result(slice(h * lanes, (h + 1) * lanes), rows_out[h * pitch : h * pitch + side, :].astype(BF16))


def send_kernel(
    occ_in, ids_in, tiles, virt, even, odd, send_row, near, far, lows, held,
    occ, ids, green, rows_in, rows_out, sem
):
    slots, side, flat = held.shape
    lanes, cut = 2 * side, even.shape[2]
    high = flat // lanes
    rows = occ.shape[0]
    first_in = pltpu.make_async_copy(occ_in, occ, sem.at[slots + 2])
    ids_copy = pltpu.make_async_copy(ids_in, ids, sem.at[slots + 3])
    first_in.start()
    ids_copy.start()
    fetch = [pltpu.make_async_copy(tiles.at[0, t], held.at[t], sem.at[t]) for t in range(slots)]
    for copy in fetch:
        copy.start()
    start = jnp.where(sends_up(), rows - 2, 0)
    row_copy = pltpu.make_async_copy(virt.at[pl.ds(start, 2)], send_row, sem.at[slots])
    near_copy = pltpu.make_async_copy(virt.at[pl.ds(0, 2)], near, sem.at[slots + 4])
    far_copy = pltpu.make_async_copy(virt.at[pl.ds(rows - 3, 3)], far, sem.at[slots + 5])
    edges = [row_copy, near_copy, far_copy]
    for copy in edges:
        copy.start()
    group = lax.axis_index("grp")
    first = lax.axis_index("mem") * rows
    odd_one = is_odd()
    source = lax.broadcasted_iota(jnp.int32, (lanes, side), 0)
    target = lax.broadcasted_iota(jnp.int32, (lanes, side), 1)
    mu = lax.rem(source, side)
    some = high // 2
    first_in.wait()
    for end, row in enumerate((0, rows - 1)):
        line = occ[row : row + 1, :].astype(F32)
        block = jnp.concatenate([line[:, h * lanes : (h + 1) * lanes] for h in range(high)], axis=0)
        for parity in range(2):
            other = (lax.rem(mu, 2) != parity).astype(jnp.int32)
            pick = (source // side == parity) & (target == mu // 2 + other * high)
            chosen = jnp.dot(
                block.astype(BF16), pick.astype(BF16), preferred_element_type=F32
            ).astype(BF16)
            for part in range(2):
                green[end, part, parity * some : (parity + 1) * some, :] = chosen[part * some : (part + 1) * some]
    ids_copy.wait()
    for t in range(slots):
        fetch[t].wait()
        end = (ids[group, 1, t] != first).astype(jnp.int32)
        lows[t] = green[end, 0]
        block = green[end, 1]

        def result(at, done):
            raw = held[t, :, at]
            even[t, :, at] = jnp.where(odd_one, done, raw)
            odd[t, :, at] = jnp.where(odd_one, raw, done)

        go_rows(block, held.at[t], rows_in, rows_out, result)
    for copy in edges:
        copy.wait()


def half_kernel(rows, ids_in, lows, tiles, even, odd, half, pick, masks, left, place, ids, rows_in, rows_out, sem):
    slots, side, flat = half.shape
    cut = even.shape[2]
    ids_copy = pltpu.make_async_copy(ids_in, ids, sem.at[1])
    ids_copy.start()
    high_part = half.at[:, :, pl.ds(cut, flat - cut)]

    @pl.when(is_odd())
    def _():
        pltpu.make_async_copy(even, high_part, sem.at[0]).start()

    @pl.when(jnp.logical_not(is_odd()))
    def _():
        pltpu.make_async_copy(odd, high_part, sem.at[0]).start()

    for t in range(slots):

        def result(at, done):
            half[t, :, at] = done

        go_rows(lows[t], tiles.at[t], rows_in, rows_out, result)
    ids_copy.wait()
    choose(rows, ids, slots, side, pick, masks, left, place)
    pltpu.make_async_copy(even, high_part, sem.at[0]).wait()


def choose(rows, ids, slots, side, pick, masks, left, place):
    width = slots * side
    group = lax.axis_index("grp")
    last = lax.axis_size("grp") - 1
    first = lax.axis_index("mem") * rows
    count = rows * lax.axis_size("mem")

    def stacked(lines, size):
        lines = lines + [jnp.zeros_like(lines[0])] * (size - len(lines))
        return jnp.concatenate(lines, axis=0)

    line = lax.broadcasted_iota(jnp.int32, (1, pick.shape[1]), 1)
    wanted = []
    for t in range(slots):
        a, b = ids[group, 1, t], ids[group, 2, t]
        at = 2 * (jnp.where(a == first, 2, 6) + b - a)
        wanted += [at - 1, at, jnp.where(b + 1 < count, at + 1, -1)]
    pick[...] = stacked([(line == w).astype(F32) for w in wanted], pick.shape[0]).astype(BF16)

    def spread(values):
        out = jnp.full(owner.shape, values[0], jnp.int32)
        for u in range(1, slots):
            out = jnp.where(owner == u, values[u], out)
        return out

    owner = lax.broadcasted_iota(jnp.int32, (1, width), 1) // side
    ahead = lax.broadcasted_iota(jnp.int32, (side, RIB * side), 1)
    ahead = ahead - lax.broadcasted_iota(jnp.int32, (side, RIB * side), 0)
    step = jnp.where(is_odd(), -1, 1)
    for k, right in enumerate((group, group + step, group - step)):
        right = jnp.clip(right, 0, last)
        row_block = spread([jnp.where(ids[right, 3, u] > 0, ids[right, 1, u], -1) for u in range(slots)])
        col_block = spread([ids[right, 2, u] for u in range(slots)])
        lines = []
        for t in range(slots):
            same = row_block == jnp.where(ids[group, 3, t] > 0, ids[group, 1, t], -2)
            for j in range(3):
                lines.append((same & (col_block == ids[group, 2, t] + (j - 1))).astype(F32))
        masks[k] = stacked(lines, masks.shape[1])
        for u in range(slots):
            place[k, u * side : (u + 1) * side, :] = (ahead == ids[right, 0, u] * side).astype(F32).astype(BF16)
    lines = []
    for p in range(RIB):
        for t in range(slots):
            lines.append(jnp.full((1, width), (ids[group, 0, t] == p).astype(F32), F32))
    left[...] = stacked(lines, left.shape[0])


def combined(products, slots, side, k, masks, left, place):
    terms = []
    for t in range(slots):
        term = None
        for j in range(3):
            at = t * 3 + j
            block = products[at * side : (at + 1) * side, :] * masks[k, at : at + 1, :]
            term = block if term is None else term + block
        terms.append(term)
    lines = []
    for p in range(RIB):
        line = None
        for t in range(slots):
            block = terms[t] * left[p * slots + t : p * slots + t + 1, :]
            line = block if line is None else line + block
        lines.append(line)
    summed = jnp.concatenate(lines, axis=0)
    coarse = summed.astype(BF16)
    fine = (summed - coarse.astype(F32)).astype(BF16)
    return jnp.dot(coarse, place[k], preferred_element_type=F32) + jnp.dot(
        fine, place[k], preferred_element_type=F32
    )


NT = (((1,), (1,)), ((), ()))
NN = (((1,), (0,)), ((), ()))


def prepare_kernel(pick, fetched, passed, near, far, half, tiles, y_all, v_high, table, mats):
    slots, side, flat = half.shape
    cut = flat - v_high.shape[1]
    copies = WIDE // side
    own = lax.broadcasted_iota(jnp.int32, (WIDE, WIDE), 0) // side
    own = own == lax.broadcasted_iota(jnp.int32, (WIDE, WIDE), 1) // side
    own = own.astype(F32).astype(BF16)

    from_above = sends_up()
    for k in range(2):
        one, two = fetched[k].astype(F32), passed[k].astype(F32)
        table[2 * k : 2 * k + 2, :] = jnp.where(from_above, two, one)
        table[2 * k + 4 : 2 * k + 6, :] = near[k].astype(F32)
        if k == 0:
            table[14:16, :] = jnp.where(from_above, one, two)
    for k in range(3):
        table[2 * k + 8 : 2 * k + 10, :] = far[k].astype(F32)
    lanes = 2 * side
    pairs = side // 2
    line_of = lax.broadcasted_iota(jnp.int32, (side, pairs), 0) // 2
    line_of = (line_of == lax.broadcasted_iota(jnp.int32, (side, pairs), 1)).astype(F32).astype(BF16)
    even_row = lax.rem(lax.broadcasted_iota(jnp.int32, (side, lanes), 0), 2) == 0
    straight = even_row == (lax.broadcasted_iota(jnp.int32, (side, lanes), 1) < side)

    table[...] = jnp.dot(pick[...], table[...].astype(BF16), preferred_element_type=F32)

    def spread(row):
        line = table[row : row + 1, :]
        block = jnp.concatenate([line[:, h * lanes : (h + 1) * lanes] for h in range(pairs)], axis=0)
        block = jnp.dot(line_of, block.astype(BF16), preferred_element_type=F32)
        block = jnp.where(straight, block, pltpu.roll(block, side, 1)).astype(BF16)
        row = jnp.concatenate([block] * (copies // 2), axis=1)
        return jnp.concatenate([row] * copies, axis=0) * own

    for k in range(slots * 3):
        mats[k] = spread(k)

    def transform(source, low, result, dims):
        lanes = result.shape[1]
        for t in range(slots):
            x = [source[t, :, c : c + WIDE] for c in range(low, low + lanes, WIDE)]
            x = jnp.concatenate(x, axis=0)
            for j in range(3):
                y = lax.dot_general(x, mats[t * 3 + j], dims[j], preferred_element_type=F32).astype(BF16)
                at = slice((t * 3 + j) * side, (t * 3 + j + 1) * side)
                for k in range(lanes // WIDE):
                    result[at, k * WIDE : (k + 1) * WIDE] = y[k * side : (k + 1) * side]

    transform(half, 0, y_all, (NT, NN, NN))
    transform(tiles, cut, v_high, (NT, NT, NN))


def middle_kernel(masks, left, place, y_all, tiles, after, middle, products):
    slots, side, flat = tiles.shape
    products[...] = lax.dot_general(
        y_all[...], tiles[...].reshape(slots * side, flat), NT, preferred_element_type=F32
    )
    middle[...] = combined(products, slots, side, 0, masks, left, place)


def pair_kernel(odd_is_upper_group, masks, left, place, y_all, v_high, other, part, send, products):
    slots, side, cut = other.shape
    group = lax.axis_index("grp")
    last = lax.axis_size("grp") - 1
    odd_one = is_odd()
    below = odd_one if odd_is_upper_group else jnp.logical_not(odd_one)
    exists = jnp.where(below, group, last - group) > 0
    partner = other[...].reshape(slots * side, cut)

    @pl.when(exists & below)
    def _():
        products[...] = lax.dot_general(y_all[:, :cut], partner, NT, preferred_element_type=F32)

    @pl.when(exists & jnp.logical_not(below))
    def _():
        products[...] = lax.dot_general(v_high[...], partner, NT, preferred_element_type=F32)

    @pl.when(exists)
    def _():
        mine = combined(products, slots, side, 1 if odd_is_upper_group else 2, masks, left, place)
        part[...] = mine
        send[...] = mine.T.astype(BF16)

    @pl.when(jnp.logical_not(exists))
    def _():
        part[...] = jnp.zeros_like(part)
        send[...] = jnp.zeros_like(send)


def band_kernel(middle, even, odd, got_even, got_odd, band):
    side = middle.shape[1]
    odd_one = is_odd()
    with_even = (even[...] + got_even[...].astype(F32)).astype(BF16)
    with_odd = (odd[...] + got_odd[...].astype(F32)).astype(BF16)
    band[:, :side] = jnp.where(odd_one, with_even, with_odd)
    band[:, side : 2 * side] = middle[...].astype(BF16)
    band[:, 2 * side :] = jnp.where(odd_one, with_odd, with_even)


def swapped(block, parity):
    count = lax.axis_size("grp")
    pairs = [(i, i + 1) for i in range(parity, count - 1, 2)]
    return lax.ppermute(block, "grp", pairs + [(b, a) for a, b in pairs])


def params(mib):
    return pltpu.CompilerParams(vmem_limit_bytes=mib * 1024 * 1024)


def in_hbm(x):
    return pltpu.with_memory_space_constraint(x, pltpu.HBM)


def in_vmem(x):
    return pltpu.with_memory_space_constraint(x, pltpu.VMEM)


WHOLE = pl.BlockSpec(memory_space=pltpu.VMEM)


def body(tiles, tile_ids, occ_blocks, virt_blocks):
    slots, side, flat = tiles.shape[1:]
    rows = occ_blocks.shape[0]
    members = lax.axis_size("mem")
    cut = flat // 2
    width = RIB * side

    anywhere = pl.BlockSpec(memory_space=pltpu.HBM)
    pitch = side + 8
    strided = [pltpu.VMEM((flat // (2 * side) * pitch, 2 * side), F32)] * 2
    even, odd, send_row, near, far, lows, held = pl.pallas_call(
        send_kernel,
        in_specs=[anywhere] * 4,
        out_specs=[WHOLE] * 2 + [anywhere] * 3 + [WHOLE] * 2,
        out_shape=[
            jax.ShapeDtypeStruct((slots, side, cut), BF16),
            jax.ShapeDtypeStruct((slots, side, cut), BF16),
            jax.ShapeDtypeStruct((2, 2, flat), BF16),
            jax.ShapeDtypeStruct((2, 2, flat), BF16),
            jax.ShapeDtypeStruct((3, 2, flat), BF16),
            jax.ShapeDtypeStruct((slots, side // 2, side), BF16),
            jax.ShapeDtypeStruct((slots, side, flat), BF16),
        ],
        scratch_shapes=[
            pltpu.VMEM(occ_blocks.shape, BF16),
            pltpu.SMEM(tile_ids.shape, jnp.int32),
            pltpu.VMEM((2, 2, side // 2, side), BF16),
            *strided,
            pltpu.SemaphoreType.DMA((slots + 6,)),
        ],
        compiler_params=params(16),
    )(*(in_hbm(x) for x in (occ_blocks, tile_ids, tiles, virt_blocks)))
    got_odd = swapped(odd, 1)
    got_even = swapped(even, 0)

    route = []
    for g in range(lax.axis_size("grp")):
        for m in range(g % 2, members - 1, 2):
            a, b = g * members + m, g * members + m + 1
            route += [(a, b), (b, a)]
    fetched = lax.ppermute(send_row, ("grp", "mem"), route)
    macs = slots * slots * 3 * side * side * flat
    picks = -(-slots * 3 // 8) * 8
    half, pick, masks, left, place = pl.pallas_call(
        functools.partial(half_kernel, rows),
        in_specs=[anywhere, WHOLE, WHOLE] + [pl.BlockSpec(memory_space=pl.ANY)] * 2,
        out_specs=[WHOLE] * 5,
        out_shape=[
            pltpu.VMEM((slots, side, flat), BF16),
            pltpu.VMEM((picks, 16), BF16),
            pltpu.VMEM((3, picks, slots * side), F32),
            pltpu.VMEM((-(-RIB * slots // 8) * 8, slots * side), F32),
            pltpu.VMEM((3, slots * side, width), BF16),
        ],
        scratch_shapes=[pltpu.SMEM(tile_ids.shape, jnp.int32), *strided, pltpu.SemaphoreType.DMA((2,))],
        compiler_params=params(12),
        cost_estimate=pl.CostEstimate(flops=2 * macs, bytes_accessed=4 * slots * side * flat, transcendentals=0),
    )(in_hbm(tile_ids), lows, held, even, odd)
    fetched, half = lax.optimization_barrier((fetched, half))
    passed = swapped(fetched, 0)
    y_all, v_high = pl.pallas_call(
        prepare_kernel,
        in_specs=[WHOLE] * 7,
        out_specs=[WHOLE, WHOLE],
        out_shape=[
            pltpu.VMEM((slots * 3 * side, flat), BF16),
            pltpu.VMEM((slots * 3 * side, flat - cut), BF16),
        ],
        scratch_shapes=[pltpu.VMEM((16, flat), F32), pltpu.VMEM((slots * 3, WIDE, WIDE), BF16)],
        compiler_params=params(20),
        cost_estimate=pl.CostEstimate(flops=3 * macs, bytes_accessed=10 * slots * side * flat, transcendentals=0),
    )(pick, fetched, passed, near, far, half, held)
    found = [pltpu.VMEM((slots * 3 * side, slots * side), F32)]

    def coupled(got, odd_is_upper_group):
        return pl.pallas_call(
            functools.partial(pair_kernel, odd_is_upper_group),
            in_specs=[WHOLE] * 6,
            out_specs=[WHOLE] * 2,
            out_shape=[pltpu.VMEM((width, width), F32), pltpu.VMEM((width, width), BF16)],
            scratch_shapes=found,
            compiler_params=params(20),
            cost_estimate=pl.CostEstimate(flops=macs, bytes_accessed=8 * slots * side * flat, transcendentals=0),
        )(masks, left, place, y_all, v_high, got)

    part_even, out_even = coupled(got_even, True)
    back_even = swapped(out_even, 0)
    part_odd, out_odd = coupled(got_odd, False)
    back_odd = swapped(out_odd, 1)
    middle = pl.pallas_call(
        middle_kernel,
        in_specs=[WHOLE] * 5 + [pl.BlockSpec(memory_space=pl.ANY)],
        out_specs=WHOLE,
        out_shape=pltpu.VMEM((width, width), F32),
        scratch_shapes=found,
        compiler_params=params(20),
        cost_estimate=pl.CostEstimate(flops=2 * macs, bytes_accessed=8 * slots * side * flat, transcendentals=0),
    )(masks, left, place, y_all, held, out_odd)
    band = pl.pallas_call(
        band_kernel,
        in_specs=[WHOLE] * 5,
        out_specs=WHOLE,
        out_shape=jax.ShapeDtypeStruct((width, 3 * width), BF16),
        compiler_params=params(8),
    )(middle, part_even, part_odd, back_even, back_odd)
    parts = lax.all_to_all(band.reshape(members, width // members, 3 * width), "mem", 0, 0)
    return parts.astype(F32).sum(axis=0)


def solution(mesh):
    placed = (
        P("grp", "mem", None, None),
        P(None, None, "mem"),
        P("mem", None),
        P("mem", None, None),
    )
    return jax.shard_map(
        body, mesh=mesh, in_specs=placed, out_specs=P(("grp", "mem"), None), check_vma=False
    )
```

```python
import functools

import jax
import jax.numpy as jnp
from jax import lax
from jax.experimental import pallas as pl
from jax.experimental.pallas import tpu as pltpu
from jax.sharding import PartitionSpec as P

RIB = 4
WIDE = 256
F32 = jnp.float32
BF16 = jnp.bfloat16


def is_odd():
    return lax.rem(lax.axis_index("grp"), 2) == 1


def sends_up():
    return lax.rem(lax.axis_index("grp") + lax.axis_index("mem"), 2) == 0


def go_rows(block, source, rows_in, rows_out, result):
    side = source.shape[0]
    lanes = 2 * side
    high = source.shape[1] // lanes
    some = block.shape[0] // 2
    pitch = side + 8
    low = lax.broadcasted_iota(jnp.int32, (some, lanes), 1) < side
    for h in range(high):
        rows_in[h * pitch : h * pitch + side, :] = source[:, h * lanes : (h + 1) * lanes].astype(F32)
    for p in range(0, side, 2):
        one = rows_in[pl.ds(p, high, stride=pitch), :]
        two = rows_in[pl.ds(p + 1, high, stride=pitch), :]
        crossed = [pltpu.roll(one, side, 1), pltpu.roll(two, side, 1)]
        x = jnp.concatenate(
            [jnp.concatenate([one, two], axis=1), jnp.concatenate(crossed, axis=1)], axis=0
        )
        y = jnp.dot(block, x.astype(BF16), preferred_element_type=F32)
        rows_out[pl.ds(p, some, stride=pitch), :] = jnp.where(low, y[:some, :lanes], y[some:, :lanes])
        rows_out[pl.ds(p + 1, some, stride=pitch), :] = jnp.where(low, y[:some, lanes:], y[some:, lanes:])
    for h in range(some):
        result(slice(h * lanes, (h + 1) * lanes), rows_out[h * pitch : h * pitch + side, :].astype(BF16))


def send_kernel(
    occ_in, ids_in, tiles, virt, even, odd, send_row, near, far, lows, held,
    occ, ids, green, rows_in, rows_out, sem
):
    slots, side, flat = held.shape
    lanes, cut = 2 * side, even.shape[2]
    high = flat // lanes
    rows = occ.shape[0]
    first_in = pltpu.make_async_copy(occ_in, occ, sem.at[slots + 2])
    ids_copy = pltpu.make_async_copy(ids_in, ids, sem.at[slots + 3])
    first_in.start()
    ids_copy.start()
    fetch = [pltpu.make_async_copy(tiles.at[0, t], held.at[t], sem.at[t]) for t in range(slots)]
    for copy in fetch[:2]:
        copy.start()
    start = jnp.where(sends_up(), rows - 2, 0)
    row_copy = pltpu.make_async_copy(virt.at[pl.ds(start, 2)], send_row, sem.at[slots])
    near_copy = pltpu.make_async_copy(virt.at[pl.ds(0, 2)], near, sem.at[slots + 4])
    far_copy = pltpu.make_async_copy(virt.at[pl.ds(rows - 3, 3)], far, sem.at[slots + 5])
    edges = [row_copy, near_copy, far_copy]
    group = lax.axis_index("grp")
    first = lax.axis_index("mem") * rows
    odd_one = is_odd()
    source = lax.broadcasted_iota(jnp.int32, (lanes, side), 0)
    target = lax.broadcasted_iota(jnp.int32, (lanes, side), 1)
    mu = lax.rem(source, side)
    some = high // 2
    first_in.wait()
    for end, row in enumerate((0, rows - 1)):
        line = occ[row : row + 1, :].astype(F32)
        block = jnp.concatenate([line[:, h * lanes : (h + 1) * lanes] for h in range(high)], axis=0)
        for parity in range(2):
            other = (lax.rem(mu, 2) != parity).astype(jnp.int32)
            pick = (source // side == parity) & (target == mu // 2 + other * high)
            chosen = jnp.dot(
                block.astype(BF16), pick.astype(BF16), preferred_element_type=F32
            ).astype(BF16)
            for part in range(2):
                green[end, part, parity * some : (parity + 1) * some, :] = chosen[part * some : (part + 1) * some]
    ids_copy.wait()
    for t in range(slots):
        fetch[t].wait()
        for copy in fetch[t + 2 : t + 3] if t + 2 < slots else edges if t + 2 == slots else []:
            copy.start()
        end = (ids[group, 1, t] != first).astype(jnp.int32)
        lows[t] = green[end, 0]
        block = green[end, 1]

        def result(at, done):
            raw = held[t, :, at]
            even[t, :, at] = jnp.where(odd_one, done, raw)
            odd[t, :, at] = jnp.where(odd_one, raw, done)

        go_rows(block, held.at[t], rows_in, rows_out, result)
    for copy in edges:
        copy.wait()


def half_kernel(rows, ids_in, lows, tiles, even, odd, half, pick, masks, left, place, ids, rows_in, rows_out, sem):
    slots, side, flat = half.shape
    cut = even.shape[2]
    ids_copy = pltpu.make_async_copy(ids_in, ids, sem.at[1])
    ids_copy.start()
    high_part = half.at[:, :, pl.ds(cut, flat - cut)]

    @pl.when(is_odd())
    def _():
        pltpu.make_async_copy(even, high_part, sem.at[0]).start()

    @pl.when(jnp.logical_not(is_odd()))
    def _():
        pltpu.make_async_copy(odd, high_part, sem.at[0]).start()

    for t in range(slots):

        def result(at, done):
            half[t, :, at] = done

        go_rows(lows[t], tiles.at[t], rows_in, rows_out, result)
    ids_copy.wait()
    choose(rows, ids, slots, side, pick, masks, left, place)
    pltpu.make_async_copy(even, high_part, sem.at[0]).wait()


def choose(rows, ids, slots, side, pick, masks, left, place):
    width = slots * side
    group = lax.axis_index("grp")
    last = lax.axis_size("grp") - 1
    first = lax.axis_index("mem") * rows
    count = rows * lax.axis_size("mem")

    def stacked(lines, size):
        lines = lines + [jnp.zeros_like(lines[0])] * (size - len(lines))
        return jnp.concatenate(lines, axis=0)

    line = lax.broadcasted_iota(jnp.int32, (1, pick.shape[1]), 1)
    wanted = []
    for t in range(slots):
        a, b = ids[group, 1, t], ids[group, 2, t]
        at = 2 * (jnp.where(a == first, 2, 6) + b - a)
        wanted += [at - 1, at, jnp.where(b + 1 < count, at + 1, -1)]
    pick[...] = stacked([(line == w).astype(F32) for w in wanted], pick.shape[0]).astype(BF16)

    def spread(values):
        out = jnp.full(owner.shape, values[0], jnp.int32)
        for u in range(1, slots):
            out = jnp.where(owner == u, values[u], out)
        return out

    owner = lax.broadcasted_iota(jnp.int32, (1, width), 1) // side
    ahead = lax.broadcasted_iota(jnp.int32, (side, RIB * side), 1)
    ahead = ahead - lax.broadcasted_iota(jnp.int32, (side, RIB * side), 0)
    step = jnp.where(is_odd(), -1, 1)
    for k, right in enumerate((group, group + step, group - step)):
        right = jnp.clip(right, 0, last)
        row_block = spread([jnp.where(ids[right, 3, u] > 0, ids[right, 1, u], -1) for u in range(slots)])
        col_block = spread([ids[right, 2, u] for u in range(slots)])
        lines = []
        for t in range(slots):
            same = row_block == jnp.where(ids[group, 3, t] > 0, ids[group, 1, t], -2)
            for j in range(3):
                lines.append((same & (col_block == ids[group, 2, t] + (j - 1))).astype(F32))
        masks[k] = stacked(lines, masks.shape[1])
        for u in range(slots):
            place[k, u * side : (u + 1) * side, :] = (ahead == ids[right, 0, u] * side).astype(F32).astype(BF16)
    lines = []
    for p in range(RIB):
        for t in range(slots):
            lines.append(jnp.full((1, width), (ids[group, 0, t] == p).astype(F32), F32))
    left[...] = stacked(lines, left.shape[0])


def combined(products, slots, side, k, masks, left, place):
    terms = []
    for t in range(slots):
        term = None
        for j in range(3):
            at = t * 3 + j
            block = products[at * side : (at + 1) * side, :] * masks[k, at : at + 1, :]
            term = block if term is None else term + block
        terms.append(term)
    lines = []
    for p in range(RIB):
        line = None
        for t in range(slots):
            block = terms[t] * left[p * slots + t : p * slots + t + 1, :]
            line = block if line is None else line + block
        lines.append(line)
    summed = jnp.concatenate(lines, axis=0)
    coarse = summed.astype(BF16)
    fine = (summed - coarse.astype(F32)).astype(BF16)
    return jnp.dot(coarse, place[k], preferred_element_type=F32) + jnp.dot(
        fine, place[k], preferred_element_type=F32
    )


NT = (((1,), (1,)), ((), ()))
NN = (((1,), (0,)), ((), ()))


def prepare_kernel(pick, fetched, passed, near, far, half, tiles, y_all, v_high, table, mats):
    slots, side, flat = half.shape
    cut = flat - v_high.shape[1]
    copies = WIDE // side
    own = lax.broadcasted_iota(jnp.int32, (WIDE, WIDE), 0) // side
    own = own == lax.broadcasted_iota(jnp.int32, (WIDE, WIDE), 1) // side
    own = own.astype(F32).astype(BF16)

    from_above = sends_up()
    for k in range(2):
        one, two = fetched[k].astype(F32), passed[k].astype(F32)
        table[2 * k : 2 * k + 2, :] = jnp.where(from_above, two, one)
        table[2 * k + 4 : 2 * k + 6, :] = near[k].astype(F32)
        if k == 0:
            table[14:16, :] = jnp.where(from_above, one, two)
    for k in range(3):
        table[2 * k + 8 : 2 * k + 10, :] = far[k].astype(F32)
    lanes = 2 * side
    pairs = side // 2
    line_of = lax.broadcasted_iota(jnp.int32, (side, pairs), 0) // 2
    line_of = (line_of == lax.broadcasted_iota(jnp.int32, (side, pairs), 1)).astype(F32).astype(BF16)
    even_row = lax.rem(lax.broadcasted_iota(jnp.int32, (side, lanes), 0), 2) == 0
    straight = even_row == (lax.broadcasted_iota(jnp.int32, (side, lanes), 1) < side)

    table[...] = jnp.dot(pick[...], table[...].astype(BF16), preferred_element_type=F32)

    def spread(row):
        line = table[row : row + 1, :]
        block = jnp.concatenate([line[:, h * lanes : (h + 1) * lanes] for h in range(pairs)], axis=0)
        block = jnp.dot(line_of, block.astype(BF16), preferred_element_type=F32)
        block = jnp.where(straight, block, pltpu.roll(block, side, 1)).astype(BF16)
        row = jnp.concatenate([block] * (copies // 2), axis=1)
        return jnp.concatenate([row] * copies, axis=0) * own

    for k in range(slots * 3):
        mats[k] = spread(k)

    def transform(source, low, result, dims):
        lanes = result.shape[1]
        for t in range(slots):
            x = [source[t, :, c : c + WIDE] for c in range(low, low + lanes, WIDE)]
            x = jnp.concatenate(x, axis=0)
            for j in range(3):
                y = lax.dot_general(x, mats[t * 3 + j], dims[j], preferred_element_type=F32).astype(BF16)
                at = slice((t * 3 + j) * side, (t * 3 + j + 1) * side)
                for k in range(lanes // WIDE):
                    result[at, k * WIDE : (k + 1) * WIDE] = y[k * side : (k + 1) * side]

    transform(half, 0, y_all, (NT, NN, NN))
    transform(tiles, cut, v_high, (NT, NT, NN))


def middle_kernel(masks, left, place, y_all, tiles, after, middle, products):
    slots, side, flat = tiles.shape
    products[...] = lax.dot_general(
        y_all[...], tiles[...].reshape(slots * side, flat), NT, preferred_element_type=F32
    )
    middle[...] = combined(products, slots, side, 0, masks, left, place)


def pair_kernel(odd_is_upper_group, masks, left, place, y_all, v_high, other, part, send, products):
    slots, side, cut = other.shape
    group = lax.axis_index("grp")
    last = lax.axis_size("grp") - 1
    odd_one = is_odd()
    below = odd_one if odd_is_upper_group else jnp.logical_not(odd_one)
    exists = jnp.where(below, group, last - group) > 0
    partner = other[...].reshape(slots * side, cut)

    @pl.when(exists & below)
    def _():
        products[...] = lax.dot_general(y_all[:, :cut], partner, NT, preferred_element_type=F32)

    @pl.when(exists & jnp.logical_not(below))
    def _():
        products[...] = lax.dot_general(v_high[...], partner, NT, preferred_element_type=F32)

    @pl.when(exists)
    def _():
        mine = combined(products, slots, side, 1 if odd_is_upper_group else 2, masks, left, place)
        part[...] = mine
        send[...] = mine.T.astype(BF16)

    @pl.when(jnp.logical_not(exists))
    def _():
        part[...] = jnp.zeros_like(part)
        send[...] = jnp.zeros_like(send)


def band_kernel(middle, even, odd, got_even, got_odd, band):
    side = middle.shape[1]
    odd_one = is_odd()
    with_even = (even[...] + got_even[...].astype(F32)).astype(BF16)
    with_odd = (odd[...] + got_odd[...].astype(F32)).astype(BF16)
    band[:, :side] = jnp.where(odd_one, with_even, with_odd)
    band[:, side : 2 * side] = middle[...].astype(BF16)
    band[:, 2 * side :] = jnp.where(odd_one, with_odd, with_even)


def swapped(block, parity):
    count = lax.axis_size("grp")
    pairs = [(i, i + 1) for i in range(parity, count - 1, 2)]
    return lax.ppermute(block, "grp", pairs + [(b, a) for a, b in pairs])


def params(mib):
    return pltpu.CompilerParams(vmem_limit_bytes=mib * 1024 * 1024)


def in_hbm(x):
    return pltpu.with_memory_space_constraint(x, pltpu.HBM)


def in_vmem(x):
    return pltpu.with_memory_space_constraint(x, pltpu.VMEM)


WHOLE = pl.BlockSpec(memory_space=pltpu.VMEM)


def body(tiles, tile_ids, occ_blocks, virt_blocks):
    slots, side, flat = tiles.shape[1:]
    rows = occ_blocks.shape[0]
    members = lax.axis_size("mem")
    cut = flat // 2
    width = RIB * side

    anywhere = pl.BlockSpec(memory_space=pltpu.HBM)
    pitch = side + 8
    strided = [pltpu.VMEM(((flat // (2 * side) + 1) * pitch, 2 * side), F32)] * 2
    even, odd, send_row, near, far, lows, held = pl.pallas_call(
        send_kernel,
        in_specs=[anywhere] * 4,
        out_specs=[WHOLE] * 2 + [anywhere] * 3 + [WHOLE] * 2,
        out_shape=[
            jax.ShapeDtypeStruct((slots, side, cut), BF16),
            jax.ShapeDtypeStruct((slots, side, cut), BF16),
            jax.ShapeDtypeStruct((2, 2, flat), BF16),
            jax.ShapeDtypeStruct((2, 2, flat), BF16),
            jax.ShapeDtypeStruct((3, 2, flat), BF16),
            jax.ShapeDtypeStruct((slots, side // 2, side), BF16),
            jax.ShapeDtypeStruct((slots, side, flat), BF16),
        ],
        scratch_shapes=[
            pltpu.VMEM(occ_blocks.shape, BF16),
            pltpu.SMEM(tile_ids.shape, jnp.int32),
            pltpu.VMEM((2, 2, side // 2, side), BF16),
            *strided,
            pltpu.SemaphoreType.DMA((slots + 6,)),
        ],
        compiler_params=params(16),
    )(*(in_hbm(x) for x in (occ_blocks, tile_ids, tiles, virt_blocks)))
    got_odd = swapped(odd, 1)
    got_even = swapped(even, 0)

    route = []
    for g in range(lax.axis_size("grp")):
        for m in range(g % 2, members - 1, 2):
            a, b = g * members + m, g * members + m + 1
            route += [(a, b), (b, a)]
    fetched = lax.ppermute(send_row, ("grp", "mem"), route)
    macs = slots * slots * 3 * side * side * flat
    picks = -(-slots * 3 // 8) * 8
    half, pick, masks, left, place = pl.pallas_call(
        functools.partial(half_kernel, rows),
        in_specs=[anywhere, WHOLE, WHOLE] + [pl.BlockSpec(memory_space=pl.ANY)] * 2,
        out_specs=[WHOLE] * 5,
        out_shape=[
            pltpu.VMEM((slots, side, flat), BF16),
            pltpu.VMEM((picks, 16), BF16),
            pltpu.VMEM((3, picks, slots * side), F32),
            pltpu.VMEM((-(-RIB * slots // 8) * 8, slots * side), F32),
            pltpu.VMEM((3, slots * side, width), BF16),
        ],
        scratch_shapes=[pltpu.SMEM(tile_ids.shape, jnp.int32), *strided, pltpu.SemaphoreType.DMA((2,))],
        compiler_params=params(12),
        cost_estimate=pl.CostEstimate(flops=2 * macs, bytes_accessed=4 * slots * side * flat, transcendentals=0),
    )(in_hbm(tile_ids), lows, held, even, odd)
    fetched, half = lax.optimization_barrier((fetched, half))
    passed = swapped(fetched, 0)
    y_all, v_high = pl.pallas_call(
        prepare_kernel,
        in_specs=[WHOLE] * 7,
        out_specs=[WHOLE, WHOLE],
        out_shape=[
            pltpu.VMEM((slots * 3 * side, flat), BF16),
            pltpu.VMEM((slots * 3 * side, flat - cut), BF16),
        ],
        scratch_shapes=[pltpu.VMEM((16, flat), F32), pltpu.VMEM((slots * 3, WIDE, WIDE), BF16)],
        compiler_params=params(20),
        cost_estimate=pl.CostEstimate(flops=3 * macs, bytes_accessed=10 * slots * side * flat, transcendentals=0),
    )(pick, fetched, passed, near, far, half, held)
    found = [pltpu.VMEM((slots * 3 * side, slots * side), F32)]

    def coupled(got, odd_is_upper_group):
        return pl.pallas_call(
            functools.partial(pair_kernel, odd_is_upper_group),
            in_specs=[WHOLE] * 6,
            out_specs=[WHOLE] * 2,
            out_shape=[pltpu.VMEM((width, width), F32), pltpu.VMEM((width, width), BF16)],
            scratch_shapes=found,
            compiler_params=params(20),
            cost_estimate=pl.CostEstimate(flops=macs, bytes_accessed=8 * slots * side * flat, transcendentals=0),
        )(masks, left, place, y_all, v_high, got)

    part_even, out_even = coupled(got_even, True)
    back_even = swapped(out_even, 0)
    part_odd, out_odd = coupled(got_odd, False)
    back_odd = swapped(out_odd, 1)
    middle = pl.pallas_call(
        middle_kernel,
        in_specs=[WHOLE] * 5 + [pl.BlockSpec(memory_space=pl.ANY)],
        out_specs=WHOLE,
        out_shape=pltpu.VMEM((width, width), F32),
        scratch_shapes=found,
        compiler_params=params(20),
        cost_estimate=pl.CostEstimate(flops=2 * macs, bytes_accessed=8 * slots * side * flat, transcendentals=0),
    )(masks, left, place, y_all, held, out_odd)
    band = pl.pallas_call(
        band_kernel,
        in_specs=[WHOLE] * 5,
        out_specs=WHOLE,
        out_shape=jax.ShapeDtypeStruct((width, 3 * width), BF16),
        compiler_params=params(8),
    )(middle, part_even, part_odd, back_even, back_odd)
    parts = lax.all_to_all(band.reshape(members, width // members, 3 * width), "mem", 0, 0)
    return parts.astype(F32).sum(axis=0)


def solution(mesh):
    placed = (
        P("grp", "mem", None, None),
        P(None, None, "mem"),
        P("mem", None),
        P("mem", None, None),
    )
    return jax.shard_map(
        body, mesh=mesh, in_specs=placed, out_specs=P(("grp", "mem"), None), check_vma=False
    )
```

```python
import functools

import jax
import jax.numpy as jnp
from jax import lax
from jax.experimental import pallas as pl
from jax.experimental.pallas import tpu as pltpu
from jax.sharding import PartitionSpec as P

RIB = 4
WIDE = 256
F32 = jnp.float32
BF16 = jnp.bfloat16


def is_odd():
    return lax.rem(lax.axis_index("grp"), 2) == 1


def sends_up():
    return lax.rem(lax.axis_index("grp") + lax.axis_index("mem"), 2) == 0


def go_rows(block, source, rows_in, rows_out, result):
    side = source.shape[0]
    lanes = 2 * side
    high = source.shape[1] // lanes
    some = block.shape[0] // 2
    pitch = side + 8
    low = lax.broadcasted_iota(jnp.int32, (some, lanes), 1) < side
    for h in range(high):
        rows_in[h * pitch : h * pitch + side, :] = source[:, h * lanes : (h + 1) * lanes].astype(F32)
    for p in range(0, side, 2):
        one = rows_in[pl.ds(p, high, stride=pitch), :]
        two = rows_in[pl.ds(p + 1, high, stride=pitch), :]
        crossed = [pltpu.roll(one, side, 1), pltpu.roll(two, side, 1)]
        x = jnp.concatenate(
            [jnp.concatenate([one, two], axis=1), jnp.concatenate(crossed, axis=1)], axis=0
        )
        y = jnp.dot(block, x.astype(BF16), preferred_element_type=F32)
        rows_out[pl.ds(p, some, stride=pitch), :] = jnp.where(low, y[:some, :lanes], y[some:, :lanes])
        rows_out[pl.ds(p + 1, some, stride=pitch), :] = jnp.where(low, y[:some, lanes:], y[some:, lanes:])
    for h in range(some):
        result(slice(h * lanes, (h + 1) * lanes), rows_out[h * pitch : h * pitch + side, :].astype(BF16))


def send_kernel(
    occ_in, ids_in, tiles, virt, even, odd, send_row, near, far, lows, held,
    occ, ids, green, rows_in, rows_out, sem
):
    slots, side, flat = held.shape
    lanes, cut = 2 * side, even.shape[2]
    high = flat // lanes
    rows = occ.shape[0]
    first_in = pltpu.make_async_copy(occ_in, occ, sem.at[slots + 2])
    ids_copy = pltpu.make_async_copy(ids_in, ids, sem.at[slots + 3])
    first_in.start()
    ids_copy.start()
    fetch = [pltpu.make_async_copy(tiles.at[0, t], held.at[t], sem.at[t]) for t in range(slots)]
    for copy in fetch[:2]:
        copy.start()
    start = jnp.where(sends_up(), rows - 2, 0)
    row_copy = pltpu.make_async_copy(virt.at[pl.ds(start, 2)], send_row, sem.at[slots])
    near_copy = pltpu.make_async_copy(virt.at[pl.ds(0, 2)], near, sem.at[slots + 4])
    far_copy = pltpu.make_async_copy(virt.at[pl.ds(rows - 3, 3)], far, sem.at[slots + 5])
    edges = [row_copy, near_copy, far_copy]
    group = lax.axis_index("grp")
    first = lax.axis_index("mem") * rows
    odd_one = is_odd()
    source = lax.broadcasted_iota(jnp.int32, (lanes, side), 0)
    target = lax.broadcasted_iota(jnp.int32, (lanes, side), 1)
    mu = lax.rem(source, side)
    some = high // 2
    first_in.wait()
    for end, row in enumerate((0, rows - 1)):
        line = occ[row : row + 1, :].astype(F32)
        block = jnp.concatenate([line[:, h * lanes : (h + 1) * lanes] for h in range(high)], axis=0)
        for parity in range(2):
            other = (lax.rem(mu, 2) != parity).astype(jnp.int32)
            pick = (source // side == parity) & (target == mu // 2 + other * high)
            chosen = jnp.dot(
                block.astype(BF16), pick.astype(BF16), preferred_element_type=F32
            ).astype(BF16)
            for part in range(2):
                green[end, part, parity * some : (parity + 1) * some, :] = chosen[part * some : (part + 1) * some]
    ids_copy.wait()
    for t in range(slots):
        fetch[t].wait()
        for copy in fetch[t + 2 : t + 3] if t + 2 < slots else edges if t + 2 == slots else []:
            copy.start()
        end = (ids[group, 1, t] != first).astype(jnp.int32)
        lows[t] = green[end, 0]
        block = green[end, 1]

        def result(at, done):
            raw = held[t, :, at]
            even[t, :, at] = jnp.where(odd_one, done, raw)
            odd[t, :, at] = jnp.where(odd_one, raw, done)

        go_rows(block, held.at[t], rows_in, rows_out, result)
    for copy in edges:
        copy.wait()


def half_kernel(rows, ids_in, lows, tiles, even, odd, half, pick, masks, left, place, ids, rows_in, rows_out, sem):
    slots, side, flat = half.shape
    cut = even.shape[2]
    ids_copy = pltpu.make_async_copy(ids_in, ids, sem.at[1])
    ids_copy.start()
    high_part = half.at[:, :, pl.ds(cut, flat - cut)]

    @pl.when(is_odd())
    def _():
        pltpu.make_async_copy(even, high_part, sem.at[0]).start()

    @pl.when(jnp.logical_not(is_odd()))
    def _():
        pltpu.make_async_copy(odd, high_part, sem.at[0]).start()

    for t in range(slots):

        def result(at, done):
            half[t, :, at] = done

        go_rows(lows[t], tiles.at[t], rows_in, rows_out, result)
    ids_copy.wait()
    choose(rows, ids, slots, side, pick, masks, left, place)
    pltpu.make_async_copy(even, high_part, sem.at[0]).wait()


def choose(rows, ids, slots, side, pick, masks, left, place):
    width = slots * side
    group = lax.axis_index("grp")
    last = lax.axis_size("grp") - 1
    first = lax.axis_index("mem") * rows
    count = rows * lax.axis_size("mem")

    def stacked(lines, size):
        lines = lines + [jnp.zeros_like(lines[0])] * (size - len(lines))
        return jnp.concatenate(lines, axis=0)

    line = lax.broadcasted_iota(jnp.int32, (1, pick.shape[1]), 1)
    wanted = []
    for t in range(slots):
        a, b = ids[group, 1, t], ids[group, 2, t]
        at = 2 * (jnp.where(a == first, 2, 6) + b - a)
        wanted += [at - 1, at, jnp.where(b + 1 < count, at + 1, -1)]
    pick[...] = stacked([(line == w).astype(F32) for w in wanted], pick.shape[0]).astype(BF16)

    def spread(values):
        out = jnp.full(owner.shape, values[0], jnp.int32)
        for u in range(1, slots):
            out = jnp.where(owner == u, values[u], out)
        return out

    owner = lax.broadcasted_iota(jnp.int32, (1, width), 1) // side
    ahead = lax.broadcasted_iota(jnp.int32, (side, RIB * side), 1)
    ahead = ahead - lax.broadcasted_iota(jnp.int32, (side, RIB * side), 0)
    step = jnp.where(is_odd(), -1, 1)
    for k, right in enumerate((group, group + step, group - step)):
        right = jnp.clip(right, 0, last)
        row_block = spread([jnp.where(ids[right, 3, u] > 0, ids[right, 1, u], -1) for u in range(slots)])
        col_block = spread([ids[right, 2, u] for u in range(slots)])
        lines = []
        for t in range(slots):
            same = row_block == jnp.where(ids[group, 3, t] > 0, ids[group, 1, t], -2)
            for j in range(3):
                lines.append((same & (col_block == ids[group, 2, t] + (j - 1))).astype(F32))
        masks[k] = stacked(lines, masks.shape[1])
        for u in range(slots):
            place[k, u * side : (u + 1) * side, :] = (ahead == ids[right, 0, u] * side).astype(F32).astype(BF16)
    lines = []
    for p in range(RIB):
        for t in range(slots):
            lines.append(jnp.full((1, width), (ids[group, 0, t] == p).astype(F32), F32))
    left[...] = stacked(lines, left.shape[0])


def combined(products, slots, side, k, masks, left, place):
    terms = []
    for t in range(slots):
        term = None
        for j in range(3):
            at = t * 3 + j
            block = products[at * side : (at + 1) * side, :] * masks[k, at : at + 1, :]
            term = block if term is None else term + block
        terms.append(term)
    lines = []
    for p in range(RIB):
        line = None
        for t in range(slots):
            block = terms[t] * left[p * slots + t : p * slots + t + 1, :]
            line = block if line is None else line + block
        lines.append(line)
    summed = jnp.concatenate(lines, axis=0)
    coarse = summed.astype(BF16)
    fine = (summed - coarse.astype(F32)).astype(BF16)
    return jnp.dot(coarse, place[k], preferred_element_type=F32) + jnp.dot(
        fine, place[k], preferred_element_type=F32
    )


NT = (((1,), (1,)), ((), ()))
NN = (((1,), (0,)), ((), ()))


def prepare_kernel(pick, fetched, passed, near, far, half, tiles, y_all, v_high, table, mats):
    slots, side, flat = half.shape
    cut = flat - v_high.shape[1]
    copies = WIDE // side
    own = lax.broadcasted_iota(jnp.int32, (WIDE, WIDE), 0) // side
    own = own == lax.broadcasted_iota(jnp.int32, (WIDE, WIDE), 1) // side
    own = own.astype(F32).astype(BF16)

    from_above = sends_up()
    for k in range(2):
        one, two = fetched[k].astype(F32), passed[k].astype(F32)
        table[2 * k : 2 * k + 2, :] = jnp.where(from_above, two, one)
        table[2 * k + 4 : 2 * k + 6, :] = near[k].astype(F32)
        if k == 0:
            table[14:16, :] = jnp.where(from_above, one, two)
    for k in range(3):
        table[2 * k + 8 : 2 * k + 10, :] = far[k].astype(F32)
    lanes = 2 * side
    pairs = side // 2
    line_of = lax.broadcasted_iota(jnp.int32, (side, pairs), 0) // 2
    line_of = (line_of == lax.broadcasted_iota(jnp.int32, (side, pairs), 1)).astype(F32).astype(BF16)
    even_row = lax.rem(lax.broadcasted_iota(jnp.int32, (side, lanes), 0), 2) == 0
    straight = even_row == (lax.broadcasted_iota(jnp.int32, (side, lanes), 1) < side)

    table[...] = jnp.dot(pick[...], table[...].astype(BF16), preferred_element_type=F32)

    def spread(row):
        line = table[row : row + 1, :]
        block = jnp.concatenate([line[:, h * lanes : (h + 1) * lanes] for h in range(pairs)], axis=0)
        block = jnp.dot(line_of, block.astype(BF16), preferred_element_type=F32)
        block = jnp.where(straight, block, pltpu.roll(block, side, 1)).astype(BF16)
        row = jnp.concatenate([block] * (copies // 2), axis=1)
        return jnp.concatenate([row] * copies, axis=0) * own

    for k in range(slots * 3):
        mats[k] = spread(k)

    def transform(source, low, result, dims):
        lanes = result.shape[1]
        for t in range(slots):
            x = [source[t, :, c : c + WIDE] for c in range(low, low + lanes, WIDE)]
            x = jnp.concatenate(x, axis=0)
            for j in range(3):
                y = lax.dot_general(x, mats[t * 3 + j], dims[j], preferred_element_type=F32).astype(BF16)
                at = slice((t * 3 + j) * side, (t * 3 + j + 1) * side)
                for k in range(lanes // WIDE):
                    result[at, k * WIDE : (k + 1) * WIDE] = y[k * side : (k + 1) * side]

    transform(half, 0, y_all, (NT, NN, NN))

    @pl.when(lax.axis_index("grp") < lax.axis_size("grp") - 1)
    def _():
        transform(tiles, cut, v_high, (NT, NT, NN))


def middle_kernel(masks, left, place, y_all, tiles, after, middle, products):
    slots, side, flat = tiles.shape
    products[...] = lax.dot_general(
        y_all[...], tiles[...].reshape(slots * side, flat), NT, preferred_element_type=F32
    )
    middle[...] = combined(products, slots, side, 0, masks, left, place)


def pair_kernel(odd_is_upper_group, masks, left, place, y_all, v_high, other, part, send, products):
    slots, side, cut = other.shape
    group = lax.axis_index("grp")
    last = lax.axis_size("grp") - 1
    odd_one = is_odd()
    below = odd_one if odd_is_upper_group else jnp.logical_not(odd_one)
    exists = jnp.where(below, group, last - group) > 0
    partner = other[...].reshape(slots * side, cut)

    @pl.when(exists & below)
    def _():
        products[...] = lax.dot_general(y_all[:, :cut], partner, NT, preferred_element_type=F32)

    @pl.when(exists & jnp.logical_not(below))
    def _():
        products[...] = lax.dot_general(v_high[...], partner, NT, preferred_element_type=F32)

    @pl.when(exists)
    def _():
        mine = combined(products, slots, side, 1 if odd_is_upper_group else 2, masks, left, place)
        part[...] = mine
        send[...] = mine.T.astype(BF16)

    @pl.when(jnp.logical_not(exists))
    def _():
        part[...] = jnp.zeros_like(part)
        send[...] = jnp.zeros_like(send)


def band_kernel(middle, even, odd, got_even, got_odd, band):
    side = middle.shape[1]
    odd_one = is_odd()
    with_even = (even[...] + got_even[...].astype(F32)).astype(BF16)
    with_odd = (odd[...] + got_odd[...].astype(F32)).astype(BF16)
    band[:, :side] = jnp.where(odd_one, with_even, with_odd)
    band[:, side : 2 * side] = middle[...].astype(BF16)
    band[:, 2 * side :] = jnp.where(odd_one, with_odd, with_even)


def swapped(block, parity):
    count = lax.axis_size("grp")
    pairs = [(i, i + 1) for i in range(parity, count - 1, 2)]
    return lax.ppermute(block, "grp", pairs + [(b, a) for a, b in pairs])


def params(mib):
    return pltpu.CompilerParams(vmem_limit_bytes=mib * 1024 * 1024)


def in_hbm(x):
    return pltpu.with_memory_space_constraint(x, pltpu.HBM)


def in_vmem(x):
    return pltpu.with_memory_space_constraint(x, pltpu.VMEM)


WHOLE = pl.BlockSpec(memory_space=pltpu.VMEM)


def body(tiles, tile_ids, occ_blocks, virt_blocks):
    slots, side, flat = tiles.shape[1:]
    rows = occ_blocks.shape[0]
    members = lax.axis_size("mem")
    cut = flat // 2
    width = RIB * side

    anywhere = pl.BlockSpec(memory_space=pltpu.HBM)
    pitch = side + 8
    strided = [pltpu.VMEM(((flat // (2 * side) + 1) * pitch, 2 * side), F32)] * 2
    even, odd, send_row, near, far, lows, held = pl.pallas_call(
        send_kernel,
        in_specs=[anywhere] * 4,
        out_specs=[WHOLE] * 2 + [anywhere] * 3 + [WHOLE] * 2,
        out_shape=[
            jax.ShapeDtypeStruct((slots, side, cut), BF16),
            jax.ShapeDtypeStruct((slots, side, cut), BF16),
            jax.ShapeDtypeStruct((2, 2, flat), BF16),
            jax.ShapeDtypeStruct((2, 2, flat), BF16),
            jax.ShapeDtypeStruct((3, 2, flat), BF16),
            jax.ShapeDtypeStruct((slots, side // 2, side), BF16),
            jax.ShapeDtypeStruct((slots, side, flat), BF16),
        ],
        scratch_shapes=[
            pltpu.VMEM(occ_blocks.shape, BF16),
            pltpu.SMEM(tile_ids.shape, jnp.int32),
            pltpu.VMEM((2, 2, side // 2, side), BF16),
            *strided,
            pltpu.SemaphoreType.DMA((slots + 6,)),
        ],
        compiler_params=params(16),
    )(*(in_hbm(x) for x in (occ_blocks, tile_ids, tiles, virt_blocks)))
    got_odd = swapped(odd, 1)
    got_even = swapped(even, 0)

    route = []
    for g in range(lax.axis_size("grp")):
        for m in range(g % 2, members - 1, 2):
            a, b = g * members + m, g * members + m + 1
            route += [(a, b), (b, a)]
    fetched = lax.ppermute(send_row, ("grp", "mem"), route)
    macs = slots * slots * 3 * side * side * flat
    picks = -(-slots * 3 // 8) * 8
    half, pick, masks, left, place = pl.pallas_call(
        functools.partial(half_kernel, rows),
        in_specs=[anywhere, WHOLE, WHOLE] + [pl.BlockSpec(memory_space=pl.ANY)] * 2,
        out_specs=[WHOLE] * 5,
        out_shape=[
            pltpu.VMEM((slots, side, flat), BF16),
            pltpu.VMEM((picks, 16), BF16),
            pltpu.VMEM((3, picks, slots * side), F32),
            pltpu.VMEM((-(-RIB * slots // 8) * 8, slots * side), F32),
            pltpu.VMEM((3, slots * side, width), BF16),
        ],
        scratch_shapes=[pltpu.SMEM(tile_ids.shape, jnp.int32), *strided, pltpu.SemaphoreType.DMA((2,))],
        compiler_params=params(12),
        cost_estimate=pl.CostEstimate(flops=2 * macs, bytes_accessed=4 * slots * side * flat, transcendentals=0),
    )(in_hbm(tile_ids), lows, held, even, odd)
    fetched, half = lax.optimization_barrier((fetched, half))
    passed = swapped(fetched, 0)
    y_all, v_high = pl.pallas_call(
        prepare_kernel,
        in_specs=[WHOLE] * 7,
        out_specs=[WHOLE, WHOLE],
        out_shape=[
            pltpu.VMEM((slots * 3 * side, flat), BF16),
            pltpu.VMEM((slots * 3 * side, flat - cut), BF16),
        ],
        scratch_shapes=[pltpu.VMEM((16, flat), F32), pltpu.VMEM((slots * 3, WIDE, WIDE), BF16)],
        compiler_params=params(20),
        cost_estimate=pl.CostEstimate(flops=3 * macs, bytes_accessed=10 * slots * side * flat, transcendentals=0),
    )(pick, fetched, passed, near, far, half, held)
    found = [pltpu.VMEM((slots * 3 * side, slots * side), F32)]

    def coupled(got, odd_is_upper_group):
        return pl.pallas_call(
            functools.partial(pair_kernel, odd_is_upper_group),
            in_specs=[WHOLE] * 6,
            out_specs=[WHOLE] * 2,
            out_shape=[pltpu.VMEM((width, width), F32), pltpu.VMEM((width, width), BF16)],
            scratch_shapes=found,
            compiler_params=params(20),
            cost_estimate=pl.CostEstimate(flops=macs, bytes_accessed=8 * slots * side * flat, transcendentals=0),
        )(masks, left, place, y_all, v_high, got)

    part_even, out_even = coupled(got_even, True)
    back_even = swapped(out_even, 0)
    part_odd, out_odd = coupled(got_odd, False)
    back_odd = swapped(out_odd, 1)
    middle = pl.pallas_call(
        middle_kernel,
        in_specs=[WHOLE] * 5 + [pl.BlockSpec(memory_space=pl.ANY)],
        out_specs=WHOLE,
        out_shape=pltpu.VMEM((width, width), F32),
        scratch_shapes=found,
        compiler_params=params(20),
        cost_estimate=pl.CostEstimate(flops=2 * macs, bytes_accessed=8 * slots * side * flat, transcendentals=0),
    )(masks, left, place, y_all, held, out_odd)
    band = pl.pallas_call(
        band_kernel,
        in_specs=[WHOLE] * 5,
        out_specs=WHOLE,
        out_shape=jax.ShapeDtypeStruct((width, 3 * width), BF16),
        compiler_params=params(8),
    )(middle, part_even, part_odd, back_even, back_odd)
    parts = lax.all_to_all(band.reshape(members, width // members, 3 * width), "mem", 0, 0)
    return parts.astype(F32).sum(axis=0)


def solution(mesh):
    placed = (
        P("grp", "mem", None, None),
        P(None, None, "mem"),
        P("mem", None),
        P("mem", None, None),
    )
    return jax.shard_map(
        body, mesh=mesh, in_specs=placed, out_specs=P(("grp", "mem"), None), check_vma=False
    )
```
